256 devices in a mesh: wide: 32 (over z, x_lo, core), narrow: 8 (over y, x_hi).
Axes of the slice: x: 4 (x_hi: 2, x_lo: 2; x = x_hi * 2 + x_lo), y: 4, z: 8, core: 2. Of those that a mesh axis runs over, the one named last changes fastest.
Arguments:
- resp_q: bfloat16 [8, 512, 4096], P(None, 'wide', 'narrow'), may hold values from -6 to 6
- resp_k: bfloat16 [8, 512, 4096], P(None, 'wide', 'narrow'), may hold values from -6 to 6
- resp_v: bfloat16 [8, 512, 4096], P(None, 'wide', 'narrow'), may hold values from -6 to 6
- resp_dout: bfloat16 [8, 512, 4096], P(None, 'wide', 'narrow'), may hold values from -6 to 6
- advantage: float32 [8], replicated, may hold values from -4 to 4
- resp_len: int32 [8], replicated, may hold values from 1 to 512, as said below
- prompt_k: bfloat16 [2048, 4096], P(('wide', 'narrow')), may hold values from -6 to 6
- prompt_v: bfloat16 [2048, 4096], P(('wide', 'narrow')), may hold values from -6 to 6
Outputs:
- grad_query: bfloat16 [8, 512, 4096], P(None, 'wide', 'narrow')
- grad_key: bfloat16 [8, 512, 4096], P(None, 'wide', 'narrow')
- grad_value: bfloat16 [8, 512, 4096], P(None, 'wide', 'narrow')
- prompt_grad_key: bfloat16 [2048, 4096], P(('wide', 'narrow'))
- prompt_grad_value: bfloat16 [2048, 4096], P(('wide', 'narrow'))
The draws below stay inside these ranges and needn't reach their ends.
Inputs may be any that keep to these rules, and one draw needn't show every extreme that they name: `resp_len`: in every draw some response has the full length 512.
All inputs are finite; a program needn't handle non-finite values.
Results may differ from the reference program's by a relative error of at most 0.03.
Values may be sent and summed in bfloat16 or wider, within the bound.
No kernel may reach another device: no remote copies, remote signals or barrier semaphores. Data moves between devices by JAX's collectives and lax.ppermute only.
A program may use at most 256 MiB of HBM per device.

```python
import jax
import jax.numpy as jnp
from jax import lax

HEADS = 32
HDIM = 128
RESPONSES = 8
HD = 4096
RESP = 512
PROMPT = 2048
N_WIDE = 32


def draw_resp_len(key, part):
    key = jax.random.fold_in(key, 7)
    first, second = jax.random.split(key)
    lengths = jax.random.randint(first, (RESPONSES,), 1, RESP + 1)
    which = jax.random.randint(second, (), 0, RESPONSES)
    return lengths.at[which].set(RESP).astype(jnp.int32)


def level_of(key, dims, cuts, low, high):
    level, own = 1.0, jax.random.fold_in(key, 6)
    for position, shards_of in cuts:
        draws = jnp.exp(jax.random.uniform(jax.random.fold_in(own, position), (shards_of,), jnp.float32, low / len(cuts), high / len(cuts)))
        level = level * jnp.repeat(draws, dims[position] // shards_of).reshape([-1 if axis == position else 1 for axis in range(len(dims))])
    return level


def bell_draw(own_key, shape, scale, limit, cuts=(), held_as=jnp.bfloat16):
    values = jax.random.normal(own_key, shape, jnp.float32) * scale
    if len(cuts) > 0:
        values = level_of(own_key, shape, cuts, -0.22, 0.18) * values
    return jnp.clip(values, min=-limit, max=limit).astype(held_as)


def setup_inputs(seed: int = 0) -> dict:
    streams_of = jax.random.split(jax.random.key(seed), 9)
    return {
        "resp_q": bell_draw(streams_of[0], (RESPONSES, RESP, HD), 1.0, 6.0, ((1, 32), (2, 8))),
        "resp_k": bell_draw(streams_of[1], (RESPONSES, RESP, HD), 1.0, 6.0, ((1, 32), (2, 8))),
        "resp_v": bell_draw(streams_of[2], (RESPONSES, RESP, HD), 1.0, 6.0, ((1, 32), (2, 8))),
        "resp_dout": bell_draw(streams_of[3], (RESPONSES, RESP, HD), 1.0, 6.0, ((1, 32), (2, 8))),
        "advantage": bell_draw(streams_of[4], (RESPONSES,), 1.0, 4.0, (), jnp.float32),
        "resp_len": draw_resp_len(jax.random.fold_in(streams_of[8], 71), 0),
        "prompt_k": bell_draw(streams_of[6], (PROMPT, HD), 1.0, 6.0, ((0, 256),)),
        "prompt_v": bell_draw(streams_of[7], (PROMPT, HD), 1.0, 6.0, ((0, 256),)),
    }


def reference(resp_q, resp_k, resp_v, resp_dout, advantage, resp_len, prompt_k, prompt_v):
    width = HEADS * HDIM
    block = RESP // N_WIDE
    factor = HDIM ** -0.5
    reach = 128.0 / (PROMPT + RESP)
    slopes = 2.0 ** (-8.0 * (jnp.arange(HEADS, dtype=jnp.float32) + 1.0) / HEADS) * reach
    key_pos = jnp.concatenate([jnp.arange(PROMPT, dtype=jnp.int32) - PROMPT, jnp.arange(RESP, dtype=jnp.int32)])
    query_pos = jnp.arange(RESP, dtype=jnp.int32)
    distance = (query_pos[:, None] - key_pos[None, :]).astype(jnp.float32)
    visible = key_pos[None, :] <= query_pos[:, None]

    def per_response(carry, items):
        queries, keys, values, cotangent, gain, length = items
        total = PROMPT + RESP
        all_keys = jnp.concatenate([prompt_k, keys], axis=0)
        all_values = jnp.concatenate([prompt_v, values], axis=0)
        weight = gain * (query_pos < length).astype(jnp.float32)
        query_heads = queries.reshape(RESP, HEADS, HDIM).astype(jnp.float32)
        key_heads = all_keys.reshape(total, HEADS, HDIM).astype(jnp.float32)
        value_heads = all_values.reshape(total, HEADS, HDIM).astype(jnp.float32)
        scores = jnp.einsum("qhd,khd->hqk", query_heads, key_heads) * factor
        scores = scores - slopes[:, None, None] * distance[None]
        masked = jnp.where(visible[None], scores, -jnp.inf)
        top = jnp.max(masked, axis=-1, keepdims=True)
        expo = jnp.exp(masked - top)
        probs = expo / jnp.sum(expo, axis=-1, keepdims=True)
        probs_b = probs.astype(jnp.bfloat16).astype(jnp.float32)
        grad_b = (cotangent.astype(jnp.float32) * weight[:, None]).astype(jnp.bfloat16)
        grad_heads = grad_b.reshape(RESP, HEADS, HDIM).astype(jnp.float32)
        output = jnp.einsum("hqk,khd->qhd", probs_b, value_heads)
        delta = jnp.sum(grad_heads * output, axis=-1)
        dprob = jnp.einsum("qhd,khd->hqk", grad_heads, value_heads)
        dscore = (probs * (dprob - delta.T[:, :, None]) * factor).astype(jnp.bfloat16).astype(jnp.float32)
        dquery = jnp.einsum("hqk,khd->qhd", dscore, key_heads).reshape(RESP, width).astype(jnp.bfloat16)
        prompt_dk = jnp.einsum("hqk,qhd->khd", dscore[:, :, :PROMPT], query_heads).reshape(PROMPT, width)
        prompt_dv = jnp.einsum("hqk,qhd->khd", probs_b[:, :, :PROMPT], grad_heads).reshape(PROMPT, width)
        score_blocks = dscore[:, :, PROMPT:].reshape(HEADS, N_WIDE, block, RESP)
        prob_blocks = probs_b[:, :, PROMPT:].reshape(HEADS, N_WIDE, block, RESP)
        query_blocks = query_heads.reshape(N_WIDE, block, HEADS, HDIM)
        grad_blocks = grad_heads.reshape(N_WIDE, block, HEADS, HDIM)

        def add_block(acc, index):
            acc_k, acc_v = acc
            term_k = jnp.einsum("hqk,qhd->khd", score_blocks[:, index], query_blocks[index]).reshape(RESP, width)
            term_v = jnp.einsum("hqk,qhd->khd", prob_blocks[:, index], grad_blocks[index]).reshape(RESP, width)
            acc_k = acc_k + term_k.astype(jnp.bfloat16).astype(jnp.float32)
            acc_v = acc_v + term_v.astype(jnp.bfloat16).astype(jnp.float32)
            return (acc_k, acc_v), None

        zeros_resp = jnp.zeros((RESP, width), jnp.float32)
        (resp_dk, resp_dv), _ = lax.scan(add_block, (zeros_resp, zeros_resp), jnp.arange(N_WIDE, dtype=jnp.int32))
        acc_pk, acc_pv = carry
        return (acc_pk + prompt_dk, acc_pv + prompt_dv), (dquery, resp_dk.astype(jnp.bfloat16), resp_dv.astype(jnp.bfloat16))

    zeros_prompt = jnp.zeros((PROMPT, width), jnp.float32)
    (sum_k, sum_v), (grad_query, grad_key, grad_value) = lax.scan(per_response, (zeros_prompt, zeros_prompt), (resp_q, resp_k, resp_v, resp_dout, advantage, resp_len))
    return grad_query, grad_key, grad_value, sum_k.astype(jnp.bfloat16), sum_v.astype(jnp.bfloat16)
```

```python
import functools

import jax
import jax.numpy as jnp
from jax import lax
from jax.experimental import pallas as pl
from jax.experimental.pallas import tpu as pltpu
from jax.sharding import Mesh, PartitionSpec as P

HEADS = 32
HDIM = 128
RESPONSES = 8
RESP = 512
PROMPT = 2048
BLOCK = 16
CHUNK = 256
LOG2E = 1.4426950408889634
F32 = jnp.float32
BF16 = jnp.bfloat16

AXES = ("zh", "zl", "x", "core", "narrow")
WIDE = ("zh", "zl", "x", "core")
GROUP = ("zl", "x", "core")

VMEM = pl.BlockSpec(memory_space=pltpu.VMEM)
SMEM = pl.BlockSpec(memory_space=pltpu.SMEM)
PARAMS = pltpu.CompilerParams(vmem_limit_bytes=48 * 1024 * 1024)


def pack_prompt_kernel(k_ref, v_ref, out_ref):
    keys = k_ref[...].astype(F32)
    values = v_ref[...].astype(F32)
    for zh in range(4):
        for n in range(8):
            cols = slice((n * 4 + zh) * HDIM, (n * 4 + zh + 1) * HDIM)
            both = jnp.concatenate([keys[:, cols], values[:, cols]], axis=0)
            both = both.astype(BF16)
            out_ref[zh * 16 + n] = both
            out_ref[zh * 16 + 8 + n] = both


def pack_resp_kernel(q_ref, k_ref, v_ref, o_ref, out_ref):
    for h in range(4):
        for r in range(RESPONSES):
            for i, ref in enumerate((q_ref, k_ref, v_ref, o_ref)):
                out_ref[h * 8 + r, i * BLOCK : (i + 1) * BLOCK, :] = ref[
                    r, :, h * HDIM : (h + 1) * HDIM
                ]


def dot(a, b, ca, cb):
    return lax.dot_general(a, b, (((ca,), (cb,)), ((), ())), preferred_element_type=F32)


def attn_kernel(
    adv_ref, len_ref, resp_ref, p00_ref, p01_ref, p10_ref, p11_ref,
    mine_ref, keep_ref, send_ref,
    k_s, v_s, t_s, d_s,
):
    me = lax.axis_index(GROUP)
    core = lax.axis_index("core")
    x = lax.axis_index("x")
    parts = ((p00_ref, p01_ref), (p10_ref, p11_ref))
    head = lax.axis_index("narrow") * 4 + lax.axis_index("zh")
    factor = HDIM ** -0.5
    n_prompt = PROMPT // CHUNK
    n_chunks = (PROMPT + RESP) // CHUNK

    queries = resp_ref[:, 0:BLOCK, :].reshape(RESP, HDIM)
    k_s[PROMPT:, :] = resp_ref[:, BLOCK : 2 * BLOCK, :].reshape(RESP, HDIM)
    v_s[PROMPT:, :] = resp_ref[:, 2 * BLOCK : 3 * BLOCK, :].reshape(RESP, HDIM)
    gain = adv_ref[me]
    length = len_ref[me]
    row = lax.broadcasted_iota(jnp.int32, (RESP, HDIM), 0)
    weight = jnp.where(row < length, gain, 0.0)
    cot = resp_ref[:, 3 * BLOCK : 4 * BLOCK, :].reshape(RESP, HDIM)
    grad = (cot.astype(F32) * weight).astype(BF16)

    power = jnp.full((8, HDIM), head + 1, jnp.int32).astype(F32) * (-8.0 / HEADS)
    slope = (jnp.exp2(power) * (128.0 / (PROMPT + RESP) * LOG2E))[0:1, :]
    key_row = lax.broadcasted_iota(jnp.int32, (CHUNK, HDIM), 0)
    prompt_row = ((key_row // 64) * 256 + key_row % 64 - PROMPT).astype(F32)
    resp_row = key_row.astype(F32)

    def wide4(x):
        return jnp.concatenate([x] * 4, axis=1)

    top = jnp.full((8, RESP), -jnp.inf, F32)
    for c in range(n_chunks):
        rows = slice(c * CHUNK, (c + 1) * CHUNK)
        if c < n_prompt:
            dc, dx, half = c % 2, (c // 2) % 2, c // 4
            both = parts[dc][dx][half * 32 : (half + 1) * 32].astype(F32)
            place = half * 1024 + jnp.bitwise_xor(x, dx) * 128 + jnp.bitwise_xor(core, dc) * 64
            k_s[rows, :] = both[:, 0:8, :].reshape(CHUNK, HDIM).astype(BF16)
            v_s[rows, :] = both[:, 8:16, :].reshape(CHUNK, HDIM).astype(BF16)
            bias = slope * (prompt_row + place.astype(F32))
        else:
            bias = slope * (resp_row + float((c - n_prompt) * CHUNK))
        scores = dot(k_s[rows, :], queries, 1, 1)
        t = scores * (factor * LOG2E) + wide4(bias)
        if c >= n_prompt:
            key_pos = lax.broadcasted_iota(jnp.int32, (CHUNK, RESP), 0) + (c - n_prompt) * CHUNK
            query_pos = lax.broadcasted_iota(jnp.int32, (CHUNK, RESP), 1)
            t = jnp.where(key_pos <= query_pos, t, -jnp.inf)
        t_s[rows, :] = t
        top = jnp.maximum(top, jnp.max(t.reshape(CHUNK // 8, 8, RESP), axis=0))
    top = jnp.max(top, axis=0, keepdims=True)

    total = jnp.zeros((8, RESP), F32)
    delta = jnp.zeros((8, RESP), F32)
    for c in range(n_chunks):
        rows = slice(c * CHUNK, (c + 1) * CHUNK)
        p = jnp.exp2(t_s[rows, :] - top)
        t_s[rows, :] = p
        dp = dot(v_s[rows, :], grad, 1, 1)
        d_s[rows, :] = dp
        total = total + jnp.sum(p.reshape(CHUNK // 8, 8, RESP), axis=0)
        delta = delta + jnp.sum((p * dp).reshape(CHUNK // 8, 8, RESP), axis=0)
    inv = 1.0 / jnp.sum(total, axis=0, keepdims=True)
    delta = jnp.sum(delta, axis=0, keepdims=True) * inv

    dq = jnp.zeros((HDIM, RESP), F32)
    for c in range(n_chunks):
        rows = slice(c * CHUNK, (c + 1) * CHUNK)
        p = t_s[rows, :] * inv
        ds = (p * (d_s[rows, :] - delta)).astype(BF16)
        dv = dot(p.astype(BF16), grad, 1, 0)
        dk = dot(ds, queries, 1, 0) * factor
        dq = dq + dot(k_s[rows, :], ds, 0, 0)
        if c < n_prompt:
            both = jnp.concatenate(
                [dk.reshape(CHUNK // 8, 8, HDIM), dv.reshape(CHUNK // 8, 8, HDIM)], axis=1
            ).astype(BF16)
            out = send_ref if c % 2 else keep_ref
            half = c // 4
            out[(c // 2) % 2, half * 32 : (half + 1) * 32] = both
        else:
            part = slice((c - n_prompt) * 16, (c - n_prompt + 1) * 16)
            mine_ref[part, BLOCK : 2 * BLOCK, :] = dk.reshape(16, BLOCK, HDIM).astype(BF16)
            mine_ref[part, 2 * BLOCK : 3 * BLOCK, :] = dv.reshape(16, BLOCK, HDIM).astype(BF16)
    dq = (dq * factor).T
    mine_ref[:, 0:BLOCK, :] = dq.reshape(32, BLOCK, HDIM).astype(BF16)


def add_core_kernel(keep_ref, got_ref, next_ref, send_ref):
    next_ref[...] = (keep_ref[0].astype(F32) + got_ref[0].astype(F32)).astype(BF16)
    send_ref[...] = (keep_ref[1].astype(F32) + got_ref[1].astype(F32)).astype(BF16)


def add_x_kernel(keep_ref, got_ref, out_ref):
    out_ref[...] = (keep_ref[...].astype(F32) + got_ref[...].astype(F32)).astype(BF16)


def unpack_resp_kernel(got_ref, q_ref, k_ref, v_ref):
    for h in range(4):
        for r in range(RESPONSES):
            for i, ref in enumerate((q_ref, k_ref, v_ref)):
                ref[r, :, h * HDIM : (h + 1) * HDIM] = got_ref[
                    h * 8 + r, i * BLOCK : (i + 1) * BLOCK, :
                ]


def unpack_prompt_kernel(got_ref, k_ref, v_ref):
    for zh in range(4):
        for n in range(8):
            cols = slice((n * 4 + zh) * HDIM, (n * 4 + zh + 1) * HDIM)
            both = got_ref[zh * 2, n].astype(F32) + got_ref[zh * 2 + 1, n].astype(F32)
            k_ref[:, cols] = both[0:8].astype(BF16)
            v_ref[:, cols] = both[8:16].astype(BF16)


def call(kernel, outs, n_in, scratch=(), smem=0, flops=0, bytes_accessed=1 << 20):
    return pl.pallas_call(
        kernel,
        out_shape=[jax.ShapeDtypeStruct(s, BF16) for s in outs],
        in_specs=[SMEM] * smem + [VMEM] * n_in,
        out_specs=[VMEM] * len(outs),
        scratch_shapes=list(scratch),
        compiler_params=PARAMS,
        cost_estimate=pl.CostEstimate(
            flops=flops, bytes_accessed=bytes_accessed, transcendentals=0
        ),
    )


def body(resp_q, resp_k, resp_v, resp_dout, advantage, resp_len, prompt_k, prompt_v):
    swap = [(0, 1), (1, 0)]
    (sent_p,) = call(pack_prompt_kernel, [(64, 16, HDIM)], 2)(prompt_k, prompt_v)
    p00 = lax.all_to_all(sent_p, ("zh", "zl", "narrow"), 0, 0, tiled=True)
    p01 = lax.ppermute(p00, "x", swap)
    p10 = lax.ppermute(p00, "core", swap)
    p11 = lax.ppermute(p01, "core", swap)
    (sent_r,) = call(pack_resp_kernel, [(32, 4 * BLOCK, HDIM)], 4)(
        resp_q, resp_k, resp_v, resp_dout
    )
    got_r = lax.all_to_all(sent_r, WIDE, 0, 0, tiled=True)

    keys = PROMPT + RESP
    mine, keep, send = call(
        attn_kernel,
        [(32, 3 * BLOCK, HDIM), (2, 64, 16, HDIM), (2, 64, 16, HDIM)],
        5,
        scratch=[
            pltpu.VMEM((keys, HDIM), BF16),
            pltpu.VMEM((keys, HDIM), BF16),
            pltpu.VMEM((keys, RESP), F32),
            pltpu.VMEM((keys, RESP), F32),
        ],
        smem=2,
        flops=5 * 2 * keys * RESP * HDIM,
        bytes_accessed=3 << 20,
    )(advantage, resp_len, got_r, p00, p01, p10, p11)

    got = lax.ppermute(send, "core", swap)
    keep, send = call(add_core_kernel, [(64, 16, HDIM)] * 2, 2)(keep, got)
    got = lax.ppermute(send, "x", swap)
    mine, _ = lax.optimization_barrier((mine, send))
    back = lax.all_to_all(mine, WIDE, 0, 0, tiled=True)
    (owned,) = call(add_x_kernel, [(64, 16, HDIM)], 2)(keep, got)
    owned, _ = lax.optimization_barrier((owned, back))
    owned = lax.all_to_all(owned, ("zh", "zl", "narrow"), 0, 0, tiled=True)
    grad_q, grad_k, grad_v = call(unpack_resp_kernel, [(RESPONSES, BLOCK, 4 * HDIM)] * 3, 1)(back)
    prompt_gk, prompt_gv = call(unpack_prompt_kernel, [(8, HEADS * HDIM)] * 2, 1)(
        owned.reshape(8, 8, 16, HDIM)
    )
    return grad_q, grad_k, grad_v, prompt_gk, prompt_gv


def solution(mesh):
    fine = Mesh(mesh.devices.reshape(4, 2, 2, 2, 8), AXES)
    resp = P(None, WIDE, "narrow")
    prompt = P(AXES, None)
    return jax.shard_map(
        body,
        mesh=fine,
        in_specs=(resp, resp, resp, resp, P(), P(), prompt, prompt),
        out_specs=(resp, resp, resp, prompt, prompt),
        check_vma=False,
    )
```

```python
import functools

import jax
import jax.numpy as jnp
from jax import lax
from jax.experimental import pallas as pl
from jax.experimental.pallas import tpu as pltpu
from jax.sharding import Mesh, PartitionSpec as P

HEADS = 32
HDIM = 128
RESPONSES = 8
RESP = 512
PROMPT = 2048
BLOCK = 16
CHUNK = 256
LOG2E = 1.4426950408889634
F32 = jnp.float32
BF16 = jnp.bfloat16

AXES = ("zh", "zl", "x", "core", "narrow")
WIDE = ("zh", "zl", "x", "core")
GROUP = ("zl", "x", "core")

VMEM = pl.BlockSpec(memory_space=pltpu.VMEM)
SMEM = pl.BlockSpec(memory_space=pltpu.SMEM)
PARAMS = pltpu.CompilerParams(vmem_limit_bytes=48 * 1024 * 1024)


def pack_prompt_kernel(k_ref, v_ref, out_ref):
    keys = k_ref[...].astype(F32)
    values = v_ref[...].astype(F32)
    for zh in range(4):
        for n in range(8):
            cols = slice((n * 4 + zh) * HDIM, (n * 4 + zh + 1) * HDIM)
            both = jnp.concatenate([keys[:, cols], values[:, cols]], axis=0)
            both = both.astype(BF16)
            out_ref[zh * 16 + n] = both
            out_ref[zh * 16 + 8 + n] = both


def pack_resp_kernel(q_ref, k_ref, v_ref, o_ref, out_ref):
    for h in range(4):
        for r in range(RESPONSES):
            for i, ref in enumerate((q_ref, k_ref, v_ref, o_ref)):
                out_ref[h * 8 + r, i * BLOCK : (i + 1) * BLOCK, :] = ref[
                    r, :, h * HDIM : (h + 1) * HDIM
                ]


def dot(a, b, ca, cb):
    return lax.dot_general(a, b, (((ca,), (cb,)), ((), ())), preferred_element_type=F32)


def attn_kernel(
    adv_ref, len_ref, resp_ref, p00_ref, p01_ref, p10_ref, p11_ref,
    mine_ref, keep_ref, send_ref,
    k_s, v_s, t_s, d_s,
):
    me = lax.axis_index(GROUP)
    core = lax.axis_index("core")
    x = lax.axis_index("x")
    parts = ((p00_ref, p01_ref), (p10_ref, p11_ref))
    head = lax.axis_index("narrow") * 4 + lax.axis_index("zh")
    factor = HDIM ** -0.5
    n_prompt = PROMPT // CHUNK
    n_chunks = (PROMPT + RESP) // CHUNK

    queries = resp_ref[:, 0:BLOCK, :].reshape(RESP, HDIM)
    k_s[PROMPT:, :] = resp_ref[:, BLOCK : 2 * BLOCK, :].reshape(RESP, HDIM)
    v_s[PROMPT:, :] = resp_ref[:, 2 * BLOCK : 3 * BLOCK, :].reshape(RESP, HDIM)
    gain = adv_ref[me]
    length = len_ref[me]
    row = lax.broadcasted_iota(jnp.int32, (RESP, HDIM), 0)
    weight = jnp.where(row < length, gain, 0.0)
    cot = resp_ref[:, 3 * BLOCK : 4 * BLOCK, :].reshape(RESP, HDIM)
    grad = (cot.astype(F32) * weight).astype(BF16)

    power = jnp.full((8, HDIM), head + 1, jnp.int32).astype(F32) * (-8.0 / HEADS)
    slope = (jnp.exp2(power) * (128.0 / (PROMPT + RESP) * LOG2E))[0:1, :]
    key_row = lax.broadcasted_iota(jnp.int32, (CHUNK, HDIM), 0)
    prompt_row = ((key_row // 64) * 256 + key_row % 64 - PROMPT).astype(F32)
    resp_row = key_row.astype(F32)

    def wide4(x):
        return jnp.concatenate([x] * 4, axis=1)

    top = jnp.full((8, RESP), -jnp.inf, F32)
    for c in range(n_chunks):
        rows = slice(c * CHUNK, (c + 1) * CHUNK)
        if c < n_prompt:
            dc, dx, half = c % 2, (c // 2) % 2, c // 4
            both = parts[dc][dx][half * 32 : (half + 1) * 32].astype(F32)
            place = half * 1024 + jnp.bitwise_xor(x, dx) * 128 + jnp.bitwise_xor(core, dc) * 64
            k_s[rows, :] = both[:, 0:8, :].reshape(CHUNK, HDIM).astype(BF16)
            v_s[rows, :] = both[:, 8:16, :].reshape(CHUNK, HDIM).astype(BF16)
            bias = slope * (prompt_row + place.astype(F32))
        else:
            bias = slope * (resp_row + float((c - n_prompt) * CHUNK))
        scores = dot(k_s[rows, :], queries, 1, 1)
        t = scores * (factor * LOG2E) + wide4(bias)
        if c >= n_prompt:
            key_pos = lax.broadcasted_iota(jnp.int32, (CHUNK, RESP), 0) + (c - n_prompt) * CHUNK
            query_pos = lax.broadcasted_iota(jnp.int32, (CHUNK, RESP), 1)
            t = jnp.where(key_pos <= query_pos, t, -jnp.inf)
        t_s[rows, :] = t
        top = jnp.maximum(top, jnp.max(t.reshape(CHUNK // 8, 8, RESP), axis=0))
    top = jnp.max(top, axis=0, keepdims=True)

    total = jnp.zeros((8, RESP), F32)
    delta = jnp.zeros((8, RESP), F32)
    for c in range(n_chunks):
        rows = slice(c * CHUNK, (c + 1) * CHUNK)
        p = jnp.exp2(t_s[rows, :] - top)
        t_s[rows, :] = p
        dp = dot(v_s[rows, :], grad, 1, 1)
        d_s[rows, :] = dp
        total = total + jnp.sum(p.reshape(CHUNK // 8, 8, RESP), axis=0)
        delta = delta + jnp.sum((p * dp).reshape(CHUNK // 8, 8, RESP), axis=0)
    inv = 1.0 / jnp.sum(total, axis=0, keepdims=True)
    delta = jnp.sum(delta, axis=0, keepdims=True) * inv

    dq = jnp.zeros((HDIM, RESP), F32)
    for c in range(n_chunks):
        rows = slice(c * CHUNK, (c + 1) * CHUNK)
        p = t_s[rows, :] * inv
        ds = (p * (d_s[rows, :] - delta)).astype(BF16)
        dv = dot(p.astype(BF16), grad, 1, 0)
        dk = dot(ds, queries, 1, 0) * factor
        dq = dq + dot(k_s[rows, :], ds, 0, 0)
        if c < n_prompt:
            both = jnp.concatenate(
                [dk.reshape(CHUNK // 8, 8, HDIM), dv.reshape(CHUNK // 8, 8, HDIM)], axis=1
            ).astype(BF16)
            out = send_ref if c % 2 else keep_ref
            half = c // 4
            out[(c // 2) % 2, half * 32 : (half + 1) * 32] = both
        else:
            part = slice((c - n_prompt) * 16, (c - n_prompt + 1) * 16)
            mine_ref[part, BLOCK : 2 * BLOCK, :] = dk.reshape(16, BLOCK, HDIM).astype(BF16)
            mine_ref[part, 2 * BLOCK : 3 * BLOCK, :] = dv.reshape(16, BLOCK, HDIM).astype(BF16)
    dq = (dq * factor).T
    mine_ref[:, 0:BLOCK, :] = dq.reshape(32, BLOCK, HDIM).astype(BF16)


def add_core_kernel(keep_ref, got_ref, next_ref, send_ref):
    next_ref[...] = (keep_ref[0].astype(F32) + got_ref[0].astype(F32)).astype(BF16)
    send_ref[...] = (keep_ref[1].astype(F32) + got_ref[1].astype(F32)).astype(BF16)


def add_x_kernel(keep_ref, got_ref, out_ref):
    out_ref[...] = (keep_ref[...].astype(F32) + got_ref[...].astype(F32)).astype(BF16)


def unpack_resp_kernel(got_ref, q_ref, k_ref, v_ref):
    for h in range(4):
        for r in range(RESPONSES):
            for i, ref in enumerate((q_ref, k_ref, v_ref)):
                ref[r, :, h * HDIM : (h + 1) * HDIM] = got_ref[
                    h * 8 + r, i * BLOCK : (i + 1) * BLOCK, :
                ]


def unpack_prompt_kernel(got_ref, k_ref, v_ref):
    for zh in range(4):
        for n in range(8):
            cols = slice((n * 4 + zh) * HDIM, (n * 4 + zh + 1) * HDIM)
            both = got_ref[zh * 2, n].astype(F32) + got_ref[zh * 2 + 1, n].astype(F32)
            k_ref[:, cols] = both[0:8].astype(BF16)
            v_ref[:, cols] = both[8:16].astype(BF16)


def call(kernel, outs, n_in, scratch=(), smem=0, flops=0, bytes_accessed=1 << 20):
    return pl.pallas_call(
        kernel,
        out_shape=[jax.ShapeDtypeStruct(s, BF16) for s in outs],
        in_specs=[SMEM] * smem + [VMEM] * n_in,
        out_specs=[VMEM] * len(outs),
        scratch_shapes=list(scratch),
        compiler_params=PARAMS,
        cost_estimate=pl.CostEstimate(
            flops=flops, bytes_accessed=bytes_accessed, transcendentals=0
        ),
    )


def body(resp_q, resp_k, resp_v, resp_dout, advantage, resp_len, prompt_k, prompt_v):
    swap = [(0, 1), (1, 0)]
    (sent_p,) = call(pack_prompt_kernel, [(64, 16, HDIM)], 2)(prompt_k, prompt_v)
    p00 = lax.all_to_all(sent_p, ("zh", "zl", "narrow"), 0, 0, tiled=True)
    p01 = lax.ppermute(p00, "x", swap)
    p10 = lax.ppermute(p00, "core", swap)
    p11 = lax.ppermute(p01, "core", swap)
    (sent_r,) = call(pack_resp_kernel, [(32, 4 * BLOCK, HDIM)], 4)(
        resp_q, resp_k, resp_v, resp_dout
    )
    got_r = lax.all_to_all(sent_r, WIDE, 0, 0, tiled=True)

    keys = PROMPT + RESP
    mine, keep, send = call(
        attn_kernel,
        [(32, 3 * BLOCK, HDIM), (2, 64, 16, HDIM), (2, 64, 16, HDIM)],
        5,
        scratch=[
            pltpu.VMEM((keys, HDIM), BF16),
            pltpu.VMEM((keys, HDIM), BF16),
            pltpu.VMEM((keys, RESP), F32),
            pltpu.VMEM((keys, RESP), F32),
        ],
        smem=2,
        flops=5 * 2 * keys * RESP * HDIM,
        bytes_accessed=3 << 20,
    )(advantage, resp_len, got_r, p00, p01, p10, p11)

    got = lax.ppermute(send, "core", swap)
    keep, send = call(add_core_kernel, [(64, 16, HDIM)] * 2, 2)(keep, got)
    got = lax.ppermute(send, "x", swap)
    back = lax.all_to_all(mine, WIDE, 0, 0, tiled=True)
    (owned,) = call(add_x_kernel, [(64, 16, HDIM)], 2)(keep, got)
    owned, _ = lax.optimization_barrier((owned, back))
    owned = lax.all_to_all(owned, ("zh", "zl", "narrow"), 0, 0, tiled=True)
    grad_q, grad_k, grad_v = call(unpack_resp_kernel, [(RESPONSES, BLOCK, 4 * HDIM)] * 3, 1)(back)
    prompt_gk, prompt_gv = call(unpack_prompt_kernel, [(8, HEADS * HDIM)] * 2, 1)(
        owned.reshape(8, 8, 16, HDIM)
    )
    return grad_q, grad_k, grad_v, prompt_gk, prompt_gv


def solution(mesh):
    fine = Mesh(mesh.devices.reshape(4, 2, 2, 2, 8), AXES)
    resp = P(None, WIDE, "narrow")
    prompt = P(AXES, None)
    return jax.shard_map(
        body,
        mesh=fine,
        in_specs=(resp, resp, resp, resp, P(), P(), prompt, prompt),
        out_specs=(resp, resp, resp, prompt, prompt),
        check_vma=False,
    )
```

```python
import functools

import jax
import jax.numpy as jnp
from jax import lax
from jax.experimental import pallas as pl
from jax.experimental.pallas import tpu as pltpu
from jax.sharding import Mesh, PartitionSpec as P

HEADS = 32
HDIM = 128
RESPONSES = 8
RESP = 512
PROMPT = 2048
BLOCK = 16
CHUNK = 256
LOG2E = 1.4426950408889634
F32 = jnp.float32
BF16 = jnp.bfloat16

AXES = ("zh", "zl", "x", "core", "narrow")
WIDE = ("zh", "zl", "x", "core")
GROUP = ("zl", "x", "core")

VMEM = pl.BlockSpec(memory_space=pltpu.VMEM)
SMEM = pl.BlockSpec(memory_space=pltpu.SMEM)
PARAMS = pltpu.CompilerParams(vmem_limit_bytes=48 * 1024 * 1024)


def pack_prompt_kernel(k_ref, v_ref, out_ref):
    keys = k_ref[...].astype(F32)
    values = v_ref[...].astype(F32)
    for zh in range(4):
        for n in range(8):
            cols = slice((n * 4 + zh) * HDIM, (n * 4 + zh + 1) * HDIM)
            both = jnp.concatenate([keys[:, cols], values[:, cols]], axis=0)
            both = both.astype(BF16)
            out_ref[zh * 16 + n] = both
            out_ref[zh * 16 + 8 + n] = both


def pack_resp_kernel(q_ref, k_ref, v_ref, o_ref, out_ref):
    for h in range(4):
        for r in range(RESPONSES):
            for i, ref in enumerate((q_ref, k_ref, v_ref, o_ref)):
                out_ref[h * 8 + r, i * BLOCK : (i + 1) * BLOCK, :] = ref[
                    r, :, h * HDIM : (h + 1) * HDIM
                ]


def dot(a, b, ca, cb):
    return lax.dot_general(a, b, (((ca,), (cb,)), ((), ())), preferred_element_type=F32)


def attn_kernel(
    adv_ref, len_ref, resp_ref, p00_ref, p01_ref, p10_ref, p11_ref,
    mine_ref, keep_ref, send_ref,
    k_s, v_s, t_s, d_s,
):
    me = lax.axis_index(GROUP)
    core = lax.axis_index("core")
    x = lax.axis_index("x")
    parts = ((p00_ref, p01_ref), (p10_ref, p11_ref))
    head = lax.axis_index("narrow") * 4 + lax.axis_index("zh")
    factor = HDIM ** -0.5
    n_prompt = PROMPT // CHUNK
    n_chunks = (PROMPT + RESP) // CHUNK

    queries = resp_ref[:, 0:BLOCK, :].reshape(RESP, HDIM)
    k_s[PROMPT:, :] = resp_ref[:, BLOCK : 2 * BLOCK, :].reshape(RESP, HDIM)
    v_s[PROMPT:, :] = resp_ref[:, 2 * BLOCK : 3 * BLOCK, :].reshape(RESP, HDIM)
    gain = adv_ref[me]
    length = len_ref[me]
    row = lax.broadcasted_iota(jnp.int32, (RESP, HDIM), 0)
    weight = jnp.where(row < length, gain, 0.0)
    cot = resp_ref[:, 3 * BLOCK : 4 * BLOCK, :].reshape(RESP, HDIM)
    grad = (cot.astype(F32) * weight).astype(BF16)

    power = jnp.full((8, HDIM), head + 1, jnp.int32).astype(F32) * (-8.0 / HEADS)
    slope = (jnp.exp2(power) * (128.0 / (PROMPT + RESP) * LOG2E))[0:1, :]
    key_row = lax.broadcasted_iota(jnp.int32, (CHUNK, HDIM), 0)
    prompt_row = ((key_row // 64) * 256 + key_row % 64 - PROMPT).astype(F32)
    resp_row = key_row.astype(F32)

    def wide4(x):
        return jnp.concatenate([x] * 4, axis=1)

    top = jnp.full((8, RESP), -jnp.inf, F32)
    for c in range(n_chunks):
        rows = slice(c * CHUNK, (c + 1) * CHUNK)
        if c < n_prompt:
            dc, dx, half = c % 2, (c // 2) % 2, c // 4
            both = parts[dc][dx][half * 32 : (half + 1) * 32].astype(F32)
            place = half * 1024 + jnp.bitwise_xor(x, dx) * 128 + jnp.bitwise_xor(core, dc) * 64
            k_s[rows, :] = both[:, 0:8, :].reshape(CHUNK, HDIM).astype(BF16)
            v_s[rows, :] = both[:, 8:16, :].reshape(CHUNK, HDIM).astype(BF16)
            bias = slope * (prompt_row + place.astype(F32))
        else:
            bias = slope * (resp_row + float((c - n_prompt) * CHUNK))
        scores = dot(k_s[rows, :], queries, 1, 1)
        t = scores * (factor * LOG2E) + wide4(bias)
        if c >= n_prompt:
            key_pos = lax.broadcasted_iota(jnp.int32, (CHUNK, RESP), 0) + (c - n_prompt) * CHUNK
            query_pos = lax.broadcasted_iota(jnp.int32, (CHUNK, RESP), 1)
            t = jnp.where(key_pos <= query_pos, t, -jnp.inf)
        t_s[rows, :] = t
        top = jnp.maximum(top, jnp.max(t.reshape(CHUNK // 8, 8, RESP), axis=0))
    top = jnp.max(top, axis=0, keepdims=True)

    total = jnp.zeros((8, RESP), F32)
    delta = jnp.zeros((8, RESP), F32)
    for c in range(n_chunks):
        rows = slice(c * CHUNK, (c + 1) * CHUNK)
        p = jnp.exp2(t_s[rows, :] - top)
        t_s[rows, :] = p
        dp = dot(v_s[rows, :], grad, 1, 1)
        d_s[rows, :] = dp
        total = total + jnp.sum(p.reshape(CHUNK // 8, 8, RESP), axis=0)
        delta = delta + jnp.sum((p * dp).reshape(CHUNK // 8, 8, RESP), axis=0)
    inv = 1.0 / jnp.sum(total, axis=0, keepdims=True)
    delta = jnp.sum(delta, axis=0, keepdims=True) * inv

    def store_blocks(z, which, rows):
        count = rows.shape[0] // (4 * BLOCK)
        rows = rows.astype(BF16).reshape(count, 4, BLOCK, HDIM)
        for xt in range(2):
            for ct in range(2):
                mine_ref[
                    z : z + count,
                    jnp.bitwise_xor(x, xt),
                    jnp.bitwise_xor(core, ct),
                    which * BLOCK : (which + 1) * BLOCK,
                    :,
                ] = rows[:, xt * 2 + ct]

    dq = jnp.zeros((HDIM, RESP), F32)
    for c in range(n_chunks):
        rows = slice(c * CHUNK, (c + 1) * CHUNK)
        p = t_s[rows, :] * inv
        ds = (p * (d_s[rows, :] - delta)).astype(BF16)
        dv = dot(p.astype(BF16), grad, 1, 0)
        dk = dot(ds, queries, 1, 0) * factor
        dq = dq + dot(k_s[rows, :], ds, 0, 0)
        if c < n_prompt:
            both = jnp.concatenate(
                [dk.reshape(CHUNK // 8, 8, HDIM), dv.reshape(CHUNK // 8, 8, HDIM)], axis=1
            ).astype(BF16)
            out = send_ref if c % 2 else keep_ref
            half = c // 4
            out[(c // 2) % 2, half * 32 : (half + 1) * 32] = both
        else:
            store_blocks((c - n_prompt) * 4, 1, dk)
            store_blocks((c - n_prompt) * 4, 2, dv)
    store_blocks(0, 0, (dq * factor).T)


def add_core_kernel(keep_ref, got_ref, next_ref, send_ref):
    next_ref[...] = (keep_ref[0].astype(F32) + got_ref[0].astype(F32)).astype(BF16)
    send_ref[...] = (keep_ref[1].astype(F32) + got_ref[1].astype(F32)).astype(BF16)


def add_x_kernel(keep_ref, got_ref, out_ref):
    out_ref[...] = (keep_ref[...].astype(F32) + got_ref[...].astype(F32)).astype(BF16)


def split_x_kernel(got_ref, out_ref):
    out_ref[...] = got_ref[:, 1]


def split_core_kernel(got_ref, from_x_ref, out_ref):
    out_ref[0] = got_ref[:, 0, 1]
    out_ref[1] = from_x_ref[:, 1]


def unpack_resp_kernel(got_ref, from_x_ref, from_core_ref, q_ref, k_ref, v_ref):
    x, core = lax.axis_index("x"), lax.axis_index("core")
    for z in range(8):
        h = z // 2
        for dx in range(2):
            for dc in range(2):
                r = (z % 2) * 4 + jnp.bitwise_xor(x, dx) * 2 + jnp.bitwise_xor(core, dc)
                if dc:
                    rows = from_core_ref[dx, z]
                else:
                    rows = from_x_ref[z, 0] if dx else got_ref[z, 0, 0]
                for i, ref in enumerate((q_ref, k_ref, v_ref)):
                    ref[r, :, h * HDIM : (h + 1) * HDIM] = rows[i * BLOCK : (i + 1) * BLOCK]


def unpack_prompt_kernel(got_ref, k_ref, v_ref):
    for zh in range(4):
        for n in range(8):
            cols = slice((n * 4 + zh) * HDIM, (n * 4 + zh + 1) * HDIM)
            both = got_ref[zh * 2, n].astype(F32) + got_ref[zh * 2 + 1, n].astype(F32)
            k_ref[:, cols] = both[0:8].astype(BF16)
            v_ref[:, cols] = both[8:16].astype(BF16)


def call(kernel, outs, n_in, scratch=(), smem=0, params=PARAMS, flops=0, bytes_accessed=1 << 20):
    return pl.pallas_call(
        kernel,
        out_shape=[jax.ShapeDtypeStruct(s, BF16) for s in outs],
        in_specs=[SMEM] * smem + [VMEM] * n_in,
        out_specs=[VMEM] * len(outs),
        scratch_shapes=list(scratch),
        compiler_params=params,
        cost_estimate=pl.CostEstimate(
            flops=flops, bytes_accessed=bytes_accessed, transcendentals=0
        ),
    )


def body(resp_q, resp_k, resp_v, resp_dout, advantage, resp_len, prompt_k, prompt_v):
    swap = [(0, 1), (1, 0)]
    (sent_p,) = call(pack_prompt_kernel, [(64, 16, HDIM)], 2, params=None)(prompt_k, prompt_v)
    p00 = lax.all_to_all(sent_p, ("zh", "zl", "narrow"), 0, 0, tiled=True)
    p01 = lax.ppermute(p00, "x", swap)
    p10 = lax.ppermute(p00, "core", swap)
    p11 = lax.ppermute(p01, "core", swap)
    (sent_r,) = call(pack_resp_kernel, [(32, 4 * BLOCK, HDIM)], 4)(
        resp_q, resp_k, resp_v, resp_dout
    )
    got_r = lax.all_to_all(sent_r, WIDE, 0, 0, tiled=True)

    keys = PROMPT + RESP
    mine, keep, send = call(
        attn_kernel,
        [(8, 2, 2, 3 * BLOCK, HDIM), (2, 64, 16, HDIM), (2, 64, 16, HDIM)],
        5,
        scratch=[
            pltpu.VMEM((keys, HDIM), BF16),
            pltpu.VMEM((keys, HDIM), BF16),
            pltpu.VMEM((keys, RESP), F32),
            pltpu.VMEM((keys, RESP), F32),
        ],
        smem=2,
        flops=5 * 2 * keys * RESP * HDIM,
        bytes_accessed=3 << 20,
    )(advantage, resp_len, got_r, p00, p01, p10, p11)

    got = lax.ppermute(send, "core", swap)
    keep, send = call(add_core_kernel, [(64, 16, HDIM)] * 2, 2)(keep, got)
    got = lax.ppermute(send, "x", swap)
    back = lax.all_to_all(mine, ("zh", "zl"), 0, 0, tiled=True)
    (owned,) = call(add_x_kernel, [(64, 16, HDIM)], 2)(keep, got)
    owned, _ = lax.optimization_barrier((owned, back))
    owned = lax.all_to_all(owned, ("zh", "zl", "narrow"), 0, 0, tiled=True)
    (part,) = call(split_x_kernel, [(8, 2, 3 * BLOCK, HDIM)], 1)(back)
    from_x = lax.ppermute(part, "x", swap)
    (part,) = call(split_core_kernel, [(2, 8, 3 * BLOCK, HDIM)], 2)(back, from_x)
    from_core = lax.ppermute(part, "core", swap)
    grad_q, grad_k, grad_v = call(unpack_resp_kernel, [(RESPONSES, BLOCK, 4 * HDIM)] * 3, 3)(
        back, from_x, from_core
    )
    prompt_gk, prompt_gv = call(unpack_prompt_kernel, [(8, HEADS * HDIM)] * 2, 1)(
        owned.reshape(8, 8, 16, HDIM)
    )
    return grad_q, grad_k, grad_v, prompt_gk, prompt_gv


def solution(mesh):
    fine = Mesh(mesh.devices.reshape(4, 2, 2, 2, 8), AXES)
    resp = P(None, WIDE, "narrow")
    prompt = P(AXES, None)
    return jax.shard_map(
        body,
        mesh=fine,
        in_specs=(resp, resp, resp, resp, P(), P(), prompt, prompt),
        out_specs=(resp, resp, resp, prompt, prompt),
        check_vma=False,
    )
```

```python
import functools

import jax
import jax.numpy as jnp
from jax import lax
from jax.experimental import pallas as pl
from jax.experimental.pallas import tpu as pltpu
from jax.sharding import Mesh, PartitionSpec as P

HEADS = 32
HDIM = 128
RESPONSES = 8
RESP = 512
PROMPT = 2048
BLOCK = 16
CHUNK = 256
LOG2E = 1.4426950408889634
F32 = jnp.float32
BF16 = jnp.bfloat16

AXES = ("zh", "zl", "x", "core", "narrow")
WIDE = ("zh", "zl", "x", "core")
GROUP = ("zl", "x", "core")

VMEM = pl.BlockSpec(memory_space=pltpu.VMEM)
SMEM = pl.BlockSpec(memory_space=pltpu.SMEM)
PARAMS = pltpu.CompilerParams(vmem_limit_bytes=48 * 1024 * 1024)


def pack_prompt_kernel(k_ref, v_ref, out_ref):
    keys = k_ref[...].astype(F32)
    values = v_ref[...].astype(F32)
    for zh in range(4):
        for n in range(8):
            cols = slice((n * 4 + zh) * HDIM, (n * 4 + zh + 1) * HDIM)
            both = jnp.concatenate([keys[:, cols], values[:, cols]], axis=0)
            both = both.astype(BF16)
            out_ref[zh * 16 + n] = both
            out_ref[zh * 16 + 8 + n] = both


def pack_resp_kernel(q_ref, k_ref, v_ref, o_ref, out_ref):
    for h in range(4):
        for r in range(RESPONSES):
            for i, ref in enumerate((q_ref, k_ref, v_ref, o_ref)):
                out_ref[h * 8 + r, i * BLOCK : (i + 1) * BLOCK, :] = ref[
                    r, :, h * HDIM : (h + 1) * HDIM
                ]


def dot(a, b, ca, cb):
    return lax.dot_general(a, b, (((ca,), (cb,)), ((), ())), preferred_element_type=F32)


def attn_kernel(
    adv_ref, len_ref, resp_ref, p00_ref, p01_ref, p10_ref, p11_ref,
    mine_ref, keep_ref, send_ref,
    k_s, v_s, t_s, d_s,
):
    me = lax.axis_index(GROUP)
    core = lax.axis_index("core")
    x = lax.axis_index("x")
    parts = ((p00_ref, p01_ref), (p10_ref, p11_ref))
    head = lax.axis_index("narrow") * 4 + lax.axis_index("zh")
    factor = HDIM ** -0.5
    n_prompt = PROMPT // CHUNK
    n_chunks = (PROMPT + RESP) // CHUNK

    queries = resp_ref[:, 0:BLOCK, :].reshape(RESP, HDIM)
    k_s[PROMPT:, :] = resp_ref[:, BLOCK : 2 * BLOCK, :].reshape(RESP, HDIM)
    v_s[PROMPT:, :] = resp_ref[:, 2 * BLOCK : 3 * BLOCK, :].reshape(RESP, HDIM)
    gain = adv_ref[me]
    length = len_ref[me]
    row = lax.broadcasted_iota(jnp.int32, (RESP, HDIM), 0)
    weight = jnp.where(row < length, gain, 0.0)
    cot = resp_ref[:, 3 * BLOCK : 4 * BLOCK, :].reshape(RESP, HDIM)
    grad = (cot.astype(F32) * weight).astype(BF16)

    power = jnp.full((8, HDIM), head + 1, jnp.int32).astype(F32) * (-8.0 / HEADS)
    slope = (jnp.exp2(power) * (128.0 / (PROMPT + RESP) * LOG2E))[0:1, :]
    key_row = lax.broadcasted_iota(jnp.int32, (CHUNK, HDIM), 0)
    prompt_row = ((key_row // 64) * 256 + key_row % 64 - PROMPT).astype(F32)
    resp_row = key_row.astype(F32)

    def wide4(x):
        return jnp.concatenate([x] * 4, axis=1)

    top = jnp.full((8, RESP), -jnp.inf, F32)
    for c in range(n_chunks):
        rows = slice(c * CHUNK, (c + 1) * CHUNK)
        if c < n_prompt:
            dc, dx, half = c % 2, (c // 2) % 2, c // 4
            both = parts[dc][dx][half * 32 : (half + 1) * 32].astype(F32)
            place = half * 1024 + jnp.bitwise_xor(x, dx) * 128 + jnp.bitwise_xor(core, dc) * 64
            k_s[rows, :] = both[:, 0:8, :].reshape(CHUNK, HDIM).astype(BF16)
            v_s[rows, :] = both[:, 8:16, :].reshape(CHUNK, HDIM).astype(BF16)
            bias = slope * (prompt_row + place.astype(F32))
        else:
            bias = slope * (resp_row + float((c - n_prompt) * CHUNK))
        scores = dot(k_s[rows, :], queries, 1, 1)
        t = scores * (factor * LOG2E) + wide4(bias)
        if c >= n_prompt:
            key_pos = lax.broadcasted_iota(jnp.int32, (CHUNK, RESP), 0) + (c - n_prompt) * CHUNK
            query_pos = lax.broadcasted_iota(jnp.int32, (CHUNK, RESP), 1)
            t = jnp.where(key_pos <= query_pos, t, -jnp.inf)
        t_s[rows, :] = t
        top = jnp.maximum(top, jnp.max(t.reshape(CHUNK // 8, 8, RESP), axis=0))
    top = jnp.max(top, axis=0, keepdims=True)

    total = jnp.zeros((8, RESP), F32)
    delta = jnp.zeros((8, RESP), F32)
    for c in range(n_chunks):
        rows = slice(c * CHUNK, (c + 1) * CHUNK)
        p = jnp.exp2(t_s[rows, :] - top)
        t_s[rows, :] = p
        dp = dot(v_s[rows, :], grad, 1, 1)
        d_s[rows, :] = dp
        total = total + jnp.sum(p.reshape(CHUNK // 8, 8, RESP), axis=0)
        delta = delta + jnp.sum((p * dp).reshape(CHUNK // 8, 8, RESP), axis=0)
    inv = 1.0 / jnp.sum(total, axis=0, keepdims=True)
    delta = jnp.sum(delta, axis=0, keepdims=True) * inv

    def store_blocks(z, which, rows):
        count = rows.shape[0] // (4 * BLOCK)
        rows = rows.astype(BF16).reshape(count, 4, BLOCK, HDIM)
        for xt in range(2):
            for ct in range(2):
                mine_ref[
                    z : z + count,
                    ct,
                    jnp.bitwise_xor(x, xt),
                    which * BLOCK : (which + 1) * BLOCK,
                    :,
                ] = rows[:, xt * 2 + ct]

    dq = jnp.zeros((HDIM, RESP), F32)
    for c in range(n_chunks):
        rows = slice(c * CHUNK, (c + 1) * CHUNK)
        p = t_s[rows, :] * inv
        ds = (p * (d_s[rows, :] - delta)).astype(BF16)
        dv = dot(p.astype(BF16), grad, 1, 0)
        dk = dot(ds, queries, 1, 0) * factor
        dq = dq + dot(k_s[rows, :], ds, 0, 0)
        if c < n_prompt:
            both = jnp.concatenate(
                [dk.reshape(CHUNK // 8, 8, HDIM), dv.reshape(CHUNK // 8, 8, HDIM)], axis=1
            ).astype(BF16)
            out = send_ref if c % 2 else keep_ref
            half = c // 4
            out[(c // 2) % 2, half * 32 : (half + 1) * 32] = both
        else:
            store_blocks((c - n_prompt) * 4, 1, dk)
            store_blocks((c - n_prompt) * 4, 2, dv)
    store_blocks(0, 0, (dq * factor).T)


def add_core_kernel(keep_ref, got_ref, next_ref, send_ref):
    next_ref[...] = (keep_ref[0].astype(F32) + got_ref[0].astype(F32)).astype(BF16)
    send_ref[...] = (keep_ref[1].astype(F32) + got_ref[1].astype(F32)).astype(BF16)


def add_x_kernel(keep_ref, got_ref, out_ref):
    out_ref[...] = (keep_ref[...].astype(F32) + got_ref[...].astype(F32)).astype(BF16)


def split_x_kernel(got_ref, out_ref):
    out_ref[...] = got_ref[:, :, 1]


def unpack_resp_kernel(got_ref, from_x_ref, q_ref, k_ref, v_ref):
    x = lax.axis_index("x")
    for z in range(8):
        h = z // 2
        for dx in range(2):
            for c in range(2):
                r = (z % 2) * 4 + jnp.bitwise_xor(x, dx) * 2 + c
                rows = from_x_ref[z, c] if dx else got_ref[z, c, 0]
                for i, ref in enumerate((q_ref, k_ref, v_ref)):
                    ref[r, :, h * HDIM : (h + 1) * HDIM] = rows[i * BLOCK : (i + 1) * BLOCK]


def unpack_prompt_kernel(got_ref, k_ref, v_ref):
    for zh in range(4):
        for n in range(8):
            cols = slice((n * 4 + zh) * HDIM, (n * 4 + zh + 1) * HDIM)
            both = got_ref[zh * 2, n].astype(F32) + got_ref[zh * 2 + 1, n].astype(F32)
            k_ref[:, cols] = both[0:8].astype(BF16)
            v_ref[:, cols] = both[8:16].astype(BF16)


def call(kernel, outs, n_in, scratch=(), smem=0, params=PARAMS, flops=0, bytes_accessed=1 << 20):
    return pl.pallas_call(
        kernel,
        out_shape=[jax.ShapeDtypeStruct(s, BF16) for s in outs],
        in_specs=[SMEM] * smem + [VMEM] * n_in,
        out_specs=[VMEM] * len(outs),
        scratch_shapes=list(scratch),
        compiler_params=params,
        cost_estimate=pl.CostEstimate(
            flops=flops, bytes_accessed=bytes_accessed, transcendentals=0
        ),
    )


def body(resp_q, resp_k, resp_v, resp_dout, advantage, resp_len, prompt_k, prompt_v):
    swap = [(0, 1), (1, 0)]
    (sent_p,) = call(pack_prompt_kernel, [(64, 16, HDIM)], 2, params=None)(prompt_k, prompt_v)
    p00 = lax.all_to_all(sent_p, ("zh", "zl", "narrow"), 0, 0, tiled=True)
    p01 = lax.ppermute(p00, "x", swap)
    p10 = lax.ppermute(p00, "core", swap)
    p11 = lax.ppermute(p01, "core", swap)
    (sent_r,) = call(pack_resp_kernel, [(32, 4 * BLOCK, HDIM)], 4)(
        resp_q, resp_k, resp_v, resp_dout
    )
    got_r = lax.all_to_all(sent_r, WIDE, 0, 0, tiled=True)

    keys = PROMPT + RESP
    mine, keep, send = call(
        attn_kernel,
        [(8, 2, 2, 3 * BLOCK, HDIM), (2, 64, 16, HDIM), (2, 64, 16, HDIM)],
        5,
        scratch=[
            pltpu.VMEM((keys, HDIM), BF16),
            pltpu.VMEM((keys, HDIM), BF16),
            pltpu.VMEM((keys, RESP), F32),
            pltpu.VMEM((keys, RESP), F32),
        ],
        smem=2,
        flops=5 * 2 * keys * RESP * HDIM,
        bytes_accessed=3 << 20,
    )(advantage, resp_len, got_r, p00, p01, p10, p11)

    got = lax.ppermute(send, "core", swap)
    keep, send = call(add_core_kernel, [(64, 16, HDIM)] * 2, 2)(keep, got)
    got = lax.ppermute(send, "x", swap)
    back = lax.all_to_all(
        mine.reshape(16, 2, 3 * BLOCK, HDIM), ("zh", "zl", "core"), 0, 0, tiled=True
    ).reshape(8, 2, 2, 3 * BLOCK, HDIM)
    (owned,) = call(add_x_kernel, [(64, 16, HDIM)], 2)(keep, got)
    owned, _ = lax.optimization_barrier((owned, back))
    owned = lax.all_to_all(owned, ("zh", "zl", "narrow"), 0, 0, tiled=True)
    (part,) = call(split_x_kernel, [(8, 2, 3 * BLOCK, HDIM)], 1)(back)
    from_x = lax.ppermute(part, "x", swap)
    grad_q, grad_k, grad_v = call(unpack_resp_kernel, [(RESPONSES, BLOCK, 4 * HDIM)] * 3, 2)(
        back, from_x
    )
    prompt_gk, prompt_gv = call(unpack_prompt_kernel, [(8, HEADS * HDIM)] * 2, 1)(
        owned.reshape(8, 8, 16, HDIM)
    )
    return grad_q, grad_k, grad_v, prompt_gk, prompt_gv


def solution(mesh):
    fine = Mesh(mesh.devices.reshape(4, 2, 2, 2, 8), AXES)
    resp = P(None, WIDE, "narrow")
    prompt = P(AXES, None)
    return jax.shard_map(
        body,
        mesh=fine,
        in_specs=(resp, resp, resp, resp, P(), P(), prompt, prompt),
        out_specs=(resp, resp, resp, prompt, prompt),
        check_vma=False,
    )
```

```python
import functools
import math

import jax
import jax.numpy as jnp
import numpy as np
from jax import lax
from jax.experimental import pallas as pl
from jax.experimental.pallas import tpu as pltpu
from jax.sharding import Mesh, PartitionSpec as P

HEADS = 32
HDIM = 128
RESPONSES = 8
RESP = 512
PROMPT = 2048
BLOCK = 16
CHUNK = 256
FLIP_IN, FLIP_RESP, FLIP_BACK, FLIP_OUT = 32, 16, 8, 32
LOG2E = 1.4426950408889634
F32 = jnp.float32
BF16 = jnp.bfloat16

AXES = ("zh", "zl", "x", "core", "narrow")
WIDE = ("zh", "zl", "x", "core")
GROUP = ("zl", "x", "core")

VMEM = pl.BlockSpec(memory_space=pltpu.VMEM)
SMEM = pl.BlockSpec(memory_space=pltpu.SMEM)
PARAMS = pltpu.CompilerParams(vmem_limit_bytes=48 * 1024 * 1024)


def pack_prompt_kernel(k_ref, v_ref, out_ref):
    keys = k_ref[...].astype(F32)
    values = v_ref[...].astype(F32)
    for zh in range(4):
        for n in range(8):
            cols = slice((n * 4 + zh) * HDIM, (n * 4 + zh + 1) * HDIM)
            both = jnp.concatenate([keys[:, cols], values[:, cols]], axis=0)
            both = both.astype(BF16)
            out_ref[(zh * 16 + n) ^ FLIP_IN] = both
            out_ref[(zh * 16 + 8 + n) ^ FLIP_IN] = both


def pack_resp_kernel(q_ref, k_ref, v_ref, o_ref, out_ref):
    for h in range(4):
        for r in range(RESPONSES):
            for i, ref in enumerate((q_ref, k_ref, v_ref, o_ref)):
                out_ref[(h * 8 + r) ^ FLIP_RESP, i * BLOCK : (i + 1) * BLOCK, :] = ref[
                    r, :, h * HDIM : (h + 1) * HDIM
                ]


def dot(a, b, ca, cb):
    return lax.dot_general(a, b, (((ca,), (cb,)), ((), ())), preferred_element_type=F32)


def attn_kernel(
    adv_ref, len_ref, resp_ref, p00_ref, p01_ref, p10_ref, p11_ref,
    mine_ref, keep_ref, send_ref,
    k_s, v_s, t_s, d_s,
):
    me = lax.axis_index(GROUP)
    core = lax.axis_index("core")
    x = lax.axis_index("x")
    parts = ((p00_ref, p01_ref), (p10_ref, p11_ref))
    head = lax.axis_index("narrow") * 4 + lax.axis_index("zh")
    factor = HDIM ** -0.5
    n_prompt = PROMPT // CHUNK
    n_chunks = (PROMPT + RESP) // CHUNK

    def take(which):
        cols = slice(which * BLOCK, (which + 1) * BLOCK)
        low, high = (resp_ref[i : i + 16, cols, :].reshape(RESP // 2, HDIM) for i in (0, 16))
        return jnp.concatenate([high, low] if FLIP_RESP else [low, high], axis=0)

    queries = take(0)
    k_s[PROMPT:, :] = take(1)
    v_s[PROMPT:, :] = take(2)
    gain = adv_ref[me]
    length = len_ref[me]
    row = lax.broadcasted_iota(jnp.int32, (RESP, HDIM), 0)
    weight = jnp.where(row < length, gain, 0.0)
    cot = take(3)
    grad = (cot.astype(F32) * weight).astype(BF16)

    power = jnp.full((8, HDIM), head + 1, jnp.int32).astype(F32) * (-8.0 / HEADS)
    slope = (jnp.exp2(power) * (128.0 / (PROMPT + RESP) * LOG2E))[0:1, :]
    key_row = lax.broadcasted_iota(jnp.int32, (CHUNK, HDIM), 0)
    block = jnp.bitwise_xor(key_row // 8, FLIP_IN % 32)
    prompt_row = ((block // 8) * 256 + (block % 8) * 8 + key_row % 8 - PROMPT).astype(F32)
    resp_row = key_row.astype(F32)

    def wide4(x):
        return jnp.concatenate([x] * 4, axis=1)

    top = jnp.full((8, RESP), -jnp.inf, F32)
    for c in range(n_chunks):
        rows = slice(c * CHUNK, (c + 1) * CHUNK)
        if c < n_prompt:
            dc, dx, half = c % 2, (c // 2) % 2, c // 4
            both = parts[dc][dx][half * 32 : (half + 1) * 32].astype(F32)
            place = (half ^ (FLIP_IN // 32)) * 1024 + jnp.bitwise_xor(x, dx) * 128 + jnp.bitwise_xor(core, dc) * 64
            k_s[rows, :] = both[:, 0:8, :].reshape(CHUNK, HDIM).astype(BF16)
            v_s[rows, :] = both[:, 8:16, :].reshape(CHUNK, HDIM).astype(BF16)
            bias = slope * (prompt_row + place.astype(F32))
        else:
            bias = slope * (resp_row + float((c - n_prompt) * CHUNK))
        scores = dot(k_s[rows, :], queries, 1, 1)
        t = scores * (factor * LOG2E) + wide4(bias)
        if c >= n_prompt:
            key_pos = lax.broadcasted_iota(jnp.int32, (CHUNK, RESP), 0) + (c - n_prompt) * CHUNK
            query_pos = lax.broadcasted_iota(jnp.int32, (CHUNK, RESP), 1)
            t = jnp.where(key_pos <= query_pos, t, -jnp.inf)
        t_s[rows, :] = t
        top = jnp.maximum(top, jnp.max(t.reshape(CHUNK // 8, 8, RESP), axis=0))
    top = jnp.max(top, axis=0, keepdims=True)

    total = jnp.zeros((8, RESP), F32)
    delta = jnp.zeros((8, RESP), F32)
    for c in range(n_chunks):
        rows = slice(c * CHUNK, (c + 1) * CHUNK)
        p = jnp.exp2(t_s[rows, :] - top)
        t_s[rows, :] = p
        dp = dot(v_s[rows, :], grad, 1, 1)
        d_s[rows, :] = dp
        total = total + jnp.sum(p.reshape(CHUNK // 8, 8, RESP), axis=0)
        delta = delta + jnp.sum((p * dp).reshape(CHUNK // 8, 8, RESP), axis=0)
    inv = 1.0 / jnp.sum(total, axis=0, keepdims=True)
    delta = jnp.sum(delta, axis=0, keepdims=True) * inv

    def store_blocks(z, which, rows):
        count = rows.shape[0] // (4 * BLOCK)
        rows = rows.astype(BF16).reshape(count, 4, BLOCK, HDIM)
        for xt in range(2):
            for ct in range(2):
                for i in range(0, count, 4):
                    at = (z + i) ^ (FLIP_BACK // 2)
                    mine_ref[
                        at : at + 4,
                        ct,
                        jnp.bitwise_xor(x, xt),
                        which * BLOCK : (which + 1) * BLOCK,
                        :,
                    ] = rows[i : i + 4, xt * 2 + ct]

    dq = jnp.zeros((HDIM, RESP), F32)
    for c in range(n_chunks):
        rows = slice(c * CHUNK, (c + 1) * CHUNK)
        p = t_s[rows, :] * inv
        ds = (p * (d_s[rows, :] - delta)).astype(BF16)
        dv = dot(p.astype(BF16), grad, 1, 0)
        dk = dot(ds, queries, 1, 0) * factor
        dq = dq + dot(k_s[rows, :], ds, 0, 0)
        if c < n_prompt:
            both = jnp.concatenate(
                [dk.reshape(CHUNK // 8, 8, HDIM), dv.reshape(CHUNK // 8, 8, HDIM)], axis=1
            ).astype(BF16)
            out = send_ref if c % 2 else keep_ref
            half = c // 4
            out[(c // 2) % 2, half * 32 : (half + 1) * 32] = both
        else:
            store_blocks((c - n_prompt) * 4, 1, dk)
            store_blocks((c - n_prompt) * 4, 2, dv)
    store_blocks(0, 0, (dq * factor).T)


def add_core_kernel(keep_ref, got_ref, next_ref, send_ref):
    next_ref[...] = (keep_ref[0].astype(F32) + got_ref[0].astype(F32)).astype(BF16)
    send_ref[...] = (keep_ref[1].astype(F32) + got_ref[1].astype(F32)).astype(BF16)


def add_x_kernel(keep_ref, got_ref, out_ref):
    out_ref[...] = (keep_ref[...].astype(F32) + got_ref[...].astype(F32)).astype(BF16)


def split_x_kernel(got_ref, out_ref):
    out_ref[...] = got_ref[:, :, 1]


def unpack_resp_kernel(got_ref, from_x_ref, q_ref, k_ref, v_ref):
    x = lax.axis_index("x")
    for z in range(8):
        h = z // 2
        for dx in range(2):
            for c in range(2):
                r = (z % 2) * 4 + jnp.bitwise_xor(x, dx) * 2 + c
                at = z ^ (FLIP_BACK // 2)
                rows = from_x_ref[at, c] if dx else got_ref[at, c, 0]
                for i, ref in enumerate((q_ref, k_ref, v_ref)):
                    ref[r, :, h * HDIM : (h + 1) * HDIM] = rows[i * BLOCK : (i + 1) * BLOCK]


def unpack_prompt_kernel(got_ref, k_ref, v_ref):
    for zh in range(4):
        for n in range(8):
            cols = slice((n * 4 + zh) * HDIM, (n * 4 + zh + 1) * HDIM)
            both = (
                got_ref[(zh * 16 + n) ^ FLIP_OUT].astype(F32)
                + got_ref[(zh * 16 + 8 + n) ^ FLIP_OUT].astype(F32)
            )
            k_ref[:, cols] = both[0:8].astype(BF16)
            v_ref[:, cols] = both[8:16].astype(BF16)


def groups_of(axes, flip):
    sizes = dict(zip(AXES, (4, 2, 2, 2, 8)))
    ids = np.arange(256).reshape([sizes[a] for a in AXES])
    rest = [a for a in AXES if a not in axes]
    ids = ids.transpose([AXES.index(a) for a in rest + list(axes)])
    ids = ids.reshape(-1, math.prod(sizes[a] for a in axes))
    return ids[:, np.arange(ids.shape[1]) ^ flip].tolist()


def exchange(x, axes, flip):
    return lax.all_to_all(
        x, AXES, 0, 0, axis_index_groups=groups_of(axes, flip), tiled=True
    )


def call(kernel, outs, n_in, scratch=(), smem=0, params=PARAMS, flops=0, bytes_accessed=1 << 20):
    return pl.pallas_call(
        kernel,
        out_shape=[jax.ShapeDtypeStruct(s, BF16) for s in outs],
        in_specs=[SMEM] * smem + [VMEM] * n_in,
        out_specs=[VMEM] * len(outs),
        scratch_shapes=list(scratch),
        compiler_params=params,
        cost_estimate=pl.CostEstimate(
            flops=flops, bytes_accessed=bytes_accessed, transcendentals=0
        ),
    )


def body(resp_q, resp_k, resp_v, resp_dout, advantage, resp_len, prompt_k, prompt_v):
    swap = [(0, 1), (1, 0)]
    (sent_p,) = call(pack_prompt_kernel, [(64, 16, HDIM)], 2, params=None)(prompt_k, prompt_v)
    p00 = exchange(sent_p, ("zh", "zl", "narrow"), FLIP_IN)
    p01 = lax.ppermute(p00, "x", swap)
    p10 = lax.ppermute(p00, "core", swap)
    p11 = lax.ppermute(p01, "core", swap)
    (sent_r,) = call(pack_resp_kernel, [(32, 4 * BLOCK, HDIM)], 4)(
        resp_q, resp_k, resp_v, resp_dout
    )
    got_r = exchange(sent_r, WIDE, FLIP_RESP)

    keys = PROMPT + RESP
    mine, keep, send = call(
        attn_kernel,
        [(8, 2, 2, 3 * BLOCK, HDIM), (2, 64, 16, HDIM), (2, 64, 16, HDIM)],
        5,
        scratch=[
            pltpu.VMEM((keys, HDIM), BF16),
            pltpu.VMEM((keys, HDIM), BF16),
            pltpu.VMEM((keys, RESP), F32),
            pltpu.VMEM((keys, RESP), F32),
        ],
        smem=2,
        flops=5 * 2 * keys * RESP * HDIM,
        bytes_accessed=3 << 20,
    )(advantage, resp_len, got_r, p00, p01, p10, p11)

    got = lax.ppermute(send, "core", swap)
    keep, send = call(add_core_kernel, [(64, 16, HDIM)] * 2, 2)(keep, got)
    got = lax.ppermute(send, "x", swap)
    back = exchange(mine.reshape(16, 2, 3 * BLOCK, HDIM), ("zh", "zl", "core"), FLIP_BACK)
    back = back.reshape(8, 2, 2, 3 * BLOCK, HDIM)
    (owned,) = call(add_x_kernel, [(64, 16, HDIM)], 2)(keep, got)
    owned, _ = lax.optimization_barrier((owned, back))
    owned = exchange(owned, ("zh", "zl", "narrow"), FLIP_OUT)
    (part,) = call(split_x_kernel, [(8, 2, 3 * BLOCK, HDIM)], 1)(back)
    from_x = lax.ppermute(part, "x", swap)
    grad_q, grad_k, grad_v = call(unpack_resp_kernel, [(RESPONSES, BLOCK, 4 * HDIM)] * 3, 2)(
        back, from_x
    )
    prompt_gk, prompt_gv = call(unpack_prompt_kernel, [(8, HEADS * HDIM)] * 2, 1)(
        owned
    )
    return grad_q, grad_k, grad_v, prompt_gk, prompt_gv


def solution(mesh):
    fine = Mesh(mesh.devices.reshape(4, 2, 2, 2, 8), AXES)
    resp = P(None, WIDE, "narrow")
    prompt = P(AXES, None)
    return jax.shard_map(
        body,
        mesh=fine,
        in_specs=(resp, resp, resp, resp, P(), P(), prompt, prompt),
        out_specs=(resp, resp, resp, prompt, prompt),
        check_vma=False,
    )
```

```python
import functools
import math

import jax
import jax.numpy as jnp
import numpy as np
from jax import lax
from jax.experimental import pallas as pl
from jax.experimental.pallas import tpu as pltpu
from jax.sharding import Mesh, PartitionSpec as P

HEADS = 32
HDIM = 128
RESPONSES = 8
RESP = 512
PROMPT = 2048
BLOCK = 16
CHUNK = 256
FLIP_IN, FLIP_RESP, FLIP_BACK, FLIP_OUT = 36, 16, 8, 36
LOG2E = 1.4426950408889634
F32 = jnp.float32
BF16 = jnp.bfloat16

AXES = ("zh", "zl", "x", "core", "narrow")
WIDE = ("zh", "zl", "x", "core")
GROUP = ("zl", "x", "core")

VMEM = pl.BlockSpec(memory_space=pltpu.VMEM)
SMEM = pl.BlockSpec(memory_space=pltpu.SMEM)
PARAMS = pltpu.CompilerParams(vmem_limit_bytes=48 * 1024 * 1024)


def pack_prompt_kernel(k_ref, v_ref, out_ref):
    keys = k_ref[...].astype(F32)
    values = v_ref[...].astype(F32)
    for zh in range(4):
        for n in range(8):
            cols = slice((n * 4 + zh) * HDIM, (n * 4 + zh + 1) * HDIM)
            both = jnp.concatenate([keys[:, cols], values[:, cols]], axis=0)
            both = both.astype(BF16)
            out_ref[(zh * 16 + n) ^ FLIP_IN] = both
            out_ref[(zh * 16 + 8 + n) ^ FLIP_IN] = both


def pack_resp_kernel(q_ref, k_ref, v_ref, o_ref, out_ref):
    for h in range(4):
        for r in range(RESPONSES):
            for i, ref in enumerate((q_ref, k_ref, v_ref, o_ref)):
                out_ref[(h * 8 + r) ^ FLIP_RESP, i * BLOCK : (i + 1) * BLOCK, :] = ref[
                    r, :, h * HDIM : (h + 1) * HDIM
                ]


def dot(a, b, ca, cb):
    return lax.dot_general(a, b, (((ca,), (cb,)), ((), ())), preferred_element_type=F32)


def attn_kernel(
    adv_ref, len_ref, resp_ref, p00_ref, p01_ref, p10_ref, p11_ref,
    mine_ref, keep_ref, send_ref,
    k_s, v_s, t_s, d_s,
):
    me = lax.axis_index(GROUP)
    core = lax.axis_index("core")
    x = lax.axis_index("x")
    parts = ((p00_ref, p01_ref), (p10_ref, p11_ref))
    head = lax.axis_index("narrow") * 4 + lax.axis_index("zh")
    factor = HDIM ** -0.5
    n_prompt = PROMPT // CHUNK
    n_chunks = (PROMPT + RESP) // CHUNK

    def take(which):
        cols = slice(which * BLOCK, (which + 1) * BLOCK)
        low, high = (resp_ref[i : i + 16, cols, :].reshape(RESP // 2, HDIM) for i in (0, 16))
        return jnp.concatenate([high, low] if FLIP_RESP else [low, high], axis=0)

    queries = take(0)
    k_s[PROMPT:, :] = take(1)
    v_s[PROMPT:, :] = take(2)
    gain = adv_ref[me]
    length = len_ref[me]
    row = lax.broadcasted_iota(jnp.int32, (RESP, HDIM), 0)
    weight = jnp.where(row < length, gain, 0.0)
    cot = take(3)
    grad = (cot.astype(F32) * weight).astype(BF16)

    power = jnp.full((8, HDIM), head + 1, jnp.int32).astype(F32) * (-8.0 / HEADS)
    slope = (jnp.exp2(power) * (128.0 / (PROMPT + RESP) * LOG2E))[0:1, :]
    key_row = lax.broadcasted_iota(jnp.int32, (CHUNK, HDIM), 0)
    block = jnp.bitwise_xor(key_row // 8, FLIP_IN % 32)
    prompt_row = ((block // 8) * 256 + (block % 8) * 8 + key_row % 8 - PROMPT).astype(F32)
    resp_row = key_row.astype(F32)

    def wide4(x):
        return jnp.concatenate([x] * 4, axis=1)

    top = jnp.full((8, RESP), -jnp.inf, F32)
    for c in range(n_chunks):
        rows = slice(c * CHUNK, (c + 1) * CHUNK)
        if c < n_prompt:
            dc, dx, half = c % 2, (c // 2) % 2, c // 4
            both = parts[dc][dx][half * 32 : (half + 1) * 32].astype(F32)
            place = (half ^ (FLIP_IN // 32)) * 1024 + jnp.bitwise_xor(x, dx) * 128 + jnp.bitwise_xor(core, dc) * 64
            k_s[rows, :] = both[:, 0:8, :].reshape(CHUNK, HDIM).astype(BF16)
            v_s[rows, :] = both[:, 8:16, :].reshape(CHUNK, HDIM).astype(BF16)
            bias = slope * (prompt_row + place.astype(F32))
        else:
            bias = slope * (resp_row + float((c - n_prompt) * CHUNK))
        scores = dot(k_s[rows, :], queries, 1, 1)
        t = scores * (factor * LOG2E) + wide4(bias)
        if c >= n_prompt:
            key_pos = lax.broadcasted_iota(jnp.int32, (CHUNK, RESP), 0) + (c - n_prompt) * CHUNK
            query_pos = lax.broadcasted_iota(jnp.int32, (CHUNK, RESP), 1)
            t = jnp.where(key_pos <= query_pos, t, -jnp.inf)
        t_s[rows, :] = t
        top = jnp.maximum(top, jnp.max(t.reshape(CHUNK // 8, 8, RESP), axis=0))
    top = jnp.max(top, axis=0, keepdims=True)

    total = jnp.zeros((8, RESP), F32)
    delta = jnp.zeros((8, RESP), F32)
    for c in range(n_chunks):
        rows = slice(c * CHUNK, (c + 1) * CHUNK)
        p = jnp.exp2(t_s[rows, :] - top)
        t_s[rows, :] = p
        dp = dot(v_s[rows, :], grad, 1, 1)
        d_s[rows, :] = dp
        total = total + jnp.sum(p.reshape(CHUNK // 8, 8, RESP), axis=0)
        delta = delta + jnp.sum((p * dp).reshape(CHUNK // 8, 8, RESP), axis=0)
    inv = 1.0 / jnp.sum(total, axis=0, keepdims=True)
    delta = jnp.sum(delta, axis=0, keepdims=True) * inv

    def store_blocks(z, which, rows):
        count = rows.shape[0] // (4 * BLOCK)
        rows = rows.astype(BF16).reshape(count, 4, BLOCK, HDIM)
        for xt in range(2):
            for ct in range(2):
                for i in range(0, count, 4):
                    at = (z + i) ^ (FLIP_BACK // 2)
                    mine_ref[
                        at : at + 4,
                        ct,
                        jnp.bitwise_xor(x, xt),
                        which * BLOCK : (which + 1) * BLOCK,
                        :,
                    ] = rows[i : i + 4, xt * 2 + ct]

    dq = jnp.zeros((HDIM, RESP), F32)
    for c in range(n_chunks):
        rows = slice(c * CHUNK, (c + 1) * CHUNK)
        p = t_s[rows, :] * inv
        ds = (p * (d_s[rows, :] - delta)).astype(BF16)
        dv = dot(p.astype(BF16), grad, 1, 0)
        dk = dot(ds, queries, 1, 0) * factor
        dq = dq + dot(k_s[rows, :], ds, 0, 0)
        if c < n_prompt:
            both = jnp.concatenate(
                [dk.reshape(CHUNK // 8, 8, HDIM), dv.reshape(CHUNK // 8, 8, HDIM)], axis=1
            ).astype(BF16)
            out = send_ref if c % 2 else keep_ref
            half = c // 4
            out[(c // 2) % 2, half * 32 : (half + 1) * 32] = both
        else:
            store_blocks((c - n_prompt) * 4, 1, dk)
            store_blocks((c - n_prompt) * 4, 2, dv)
    store_blocks(0, 0, (dq * factor).T)


def add_core_kernel(keep_ref, got_ref, next_ref, send_ref):
    next_ref[...] = (keep_ref[0].astype(F32) + got_ref[0].astype(F32)).astype(BF16)
    send_ref[...] = (keep_ref[1].astype(F32) + got_ref[1].astype(F32)).astype(BF16)


def add_x_kernel(keep_ref, got_ref, out_ref):
    out_ref[...] = (keep_ref[...].astype(F32) + got_ref[...].astype(F32)).astype(BF16)


def split_x_kernel(got_ref, out_ref):
    out_ref[...] = got_ref[:, :, 1]


def unpack_resp_kernel(got_ref, from_x_ref, q_ref, k_ref, v_ref):
    x = lax.axis_index("x")
    for z in range(8):
        h = z // 2
        for dx in range(2):
            for c in range(2):
                r = (z % 2) * 4 + jnp.bitwise_xor(x, dx) * 2 + c
                at = z ^ (FLIP_BACK // 2)
                rows = from_x_ref[at, c] if dx else got_ref[at, c, 0]
                for i, ref in enumerate((q_ref, k_ref, v_ref)):
                    ref[r, :, h * HDIM : (h + 1) * HDIM] = rows[i * BLOCK : (i + 1) * BLOCK]


def unpack_prompt_kernel(got_ref, k_ref, v_ref):
    for zh in range(4):
        for n in range(8):
            cols = slice((n * 4 + zh) * HDIM, (n * 4 + zh + 1) * HDIM)
            both = (
                got_ref[(zh * 16 + n) ^ FLIP_OUT].astype(F32)
                + got_ref[(zh * 16 + 8 + n) ^ FLIP_OUT].astype(F32)
            )
            k_ref[:, cols] = both[0:8].astype(BF16)
            v_ref[:, cols] = both[8:16].astype(BF16)


def groups_of(axes, flip):
    sizes = dict(zip(AXES, (4, 2, 2, 2, 8)))
    ids = np.arange(256).reshape([sizes[a] for a in AXES])
    rest = [a for a in AXES if a not in axes]
    ids = ids.transpose([AXES.index(a) for a in rest + list(axes)])
    ids = ids.reshape(-1, math.prod(sizes[a] for a in axes))
    return ids[:, np.arange(ids.shape[1]) ^ flip].tolist()


def exchange(x, axes, flip):
    return lax.all_to_all(
        x, AXES, 0, 0, axis_index_groups=groups_of(axes, flip), tiled=True
    )


def call(kernel, outs, n_in, scratch=(), smem=0, params=PARAMS, flops=0, bytes_accessed=1 << 20):
    return pl.pallas_call(
        kernel,
        out_shape=[jax.ShapeDtypeStruct(s, BF16) for s in outs],
        in_specs=[SMEM] * smem + [VMEM] * n_in,
        out_specs=[VMEM] * len(outs),
        scratch_shapes=list(scratch),
        compiler_params=params,
        cost_estimate=pl.CostEstimate(
            flops=flops, bytes_accessed=bytes_accessed, transcendentals=0
        ),
    )


def body(resp_q, resp_k, resp_v, resp_dout, advantage, resp_len, prompt_k, prompt_v):
    swap = [(0, 1), (1, 0)]
    (sent_p,) = call(pack_prompt_kernel, [(64, 16, HDIM)], 2, params=None)(prompt_k, prompt_v)
    p00 = exchange(sent_p, ("zh", "zl", "narrow"), FLIP_IN)
    p01 = lax.ppermute(p00, "x", swap)
    p10 = lax.ppermute(p00, "core", swap)
    p11 = lax.ppermute(p01, "core", swap)
    (sent_r,) = call(pack_resp_kernel, [(32, 4 * BLOCK, HDIM)], 4)(
        resp_q, resp_k, resp_v, resp_dout
    )
    got_r = exchange(sent_r, WIDE, FLIP_RESP)

    keys = PROMPT + RESP
    mine, keep, send = call(
        attn_kernel,
        [(8, 2, 2, 3 * BLOCK, HDIM), (2, 64, 16, HDIM), (2, 64, 16, HDIM)],
        5,
        scratch=[
            pltpu.VMEM((keys, HDIM), BF16),
            pltpu.VMEM((keys, HDIM), BF16),
            pltpu.VMEM((keys, RESP), F32),
            pltpu.VMEM((keys, RESP), F32),
        ],
        smem=2,
        flops=5 * 2 * keys * RESP * HDIM,
        bytes_accessed=3 << 20,
    )(advantage, resp_len, got_r, p00, p01, p10, p11)

    got = lax.ppermute(send, "core", swap)
    keep, send = call(add_core_kernel, [(64, 16, HDIM)] * 2, 2)(keep, got)
    got = lax.ppermute(send, "x", swap)
    back = exchange(mine.reshape(16, 2, 3 * BLOCK, HDIM), ("zh", "zl", "core"), FLIP_BACK)
    back = back.reshape(8, 2, 2, 3 * BLOCK, HDIM)
    (owned,) = call(add_x_kernel, [(64, 16, HDIM)], 2)(keep, got)
    owned, _ = lax.optimization_barrier((owned, back))
    owned = exchange(owned, ("zh", "zl", "narrow"), FLIP_OUT)
    (part,) = call(split_x_kernel, [(8, 2, 3 * BLOCK, HDIM)], 1)(back)
    from_x = lax.ppermute(part, "x", swap)
    grad_q, grad_k, grad_v = call(unpack_resp_kernel, [(RESPONSES, BLOCK, 4 * HDIM)] * 3, 2)(
        back, from_x
    )
    prompt_gk, prompt_gv = call(unpack_prompt_kernel, [(8, HEADS * HDIM)] * 2, 1)(
        owned
    )
    return grad_q, grad_k, grad_v, prompt_gk, prompt_gv


def solution(mesh):
    fine = Mesh(mesh.devices.reshape(4, 2, 2, 2, 8), AXES)
    resp = P(None, WIDE, "narrow")
    prompt = P(AXES, None)
    return jax.shard_map(
        body,
        mesh=fine,
        in_specs=(resp, resp, resp, resp, P(), P(), prompt, prompt),
        out_specs=(resp, resp, resp, prompt, prompt),
        check_vma=False,
    )
```

```python
import functools
import math

import jax
import jax.numpy as jnp
import numpy as np
from jax import lax
from jax.experimental import pallas as pl
from jax.experimental.pallas import tpu as pltpu
from jax.sharding import Mesh, PartitionSpec as P

HEADS = 32
HDIM = 128
RESPONSES = 8
RESP = 512
PROMPT = 2048
BLOCK = 16
CHUNK = 256
FLIP_IN, FLIP_RESP, FLIP_BACK, FLIP_OUT = 37, 16, 8, 36
LOG2E = 1.4426950408889634
F32 = jnp.float32
BF16 = jnp.bfloat16

AXES = ("zh", "zl", "x", "core", "narrow")
WIDE = ("zh", "zl", "x", "core")
GROUP = ("zl", "x", "core")

VMEM = pl.BlockSpec(memory_space=pltpu.VMEM)
SMEM = pl.BlockSpec(memory_space=pltpu.SMEM)
PARAMS = pltpu.CompilerParams(vmem_limit_bytes=48 * 1024 * 1024)


def pack_prompt_kernel(k_ref, v_ref, out_ref):
    keys = k_ref[...].astype(F32)
    values = v_ref[...].astype(F32)
    for zh in range(4):
        for n in range(8):
            cols = slice((n * 4 + zh) * HDIM, (n * 4 + zh + 1) * HDIM)
            both = jnp.concatenate([keys[:, cols], values[:, cols]], axis=0)
            both = both.astype(BF16)
            out_ref[(zh * 16 + n) ^ FLIP_IN] = both
            out_ref[(zh * 16 + 8 + n) ^ FLIP_IN] = both


def pack_resp_kernel(q_ref, k_ref, v_ref, o_ref, out_ref):
    for h in range(4):
        for r in range(RESPONSES):
            for i, ref in enumerate((q_ref, k_ref, v_ref, o_ref)):
                out_ref[(h * 8 + r) ^ FLIP_RESP, i * BLOCK : (i + 1) * BLOCK, :] = ref[
                    r, :, h * HDIM : (h + 1) * HDIM
                ]


def dot(a, b, ca, cb):
    return lax.dot_general(a, b, (((ca,), (cb,)), ((), ())), preferred_element_type=F32)


def attn_kernel(
    adv_ref, len_ref, resp_ref, p00_ref, p01_ref, p10_ref, p11_ref,
    mine_ref, keep_ref, send_ref,
    k_s, v_s, t_s, d_s,
):
    me = lax.axis_index(GROUP)
    core = lax.axis_index("core")
    x = lax.axis_index("x")
    parts = ((p00_ref, p01_ref), (p10_ref, p11_ref))
    head = lax.axis_index("narrow") * 4 + lax.axis_index("zh")
    factor = HDIM ** -0.5
    n_prompt = PROMPT // CHUNK
    n_chunks = (PROMPT + RESP) // CHUNK

    def take(which):
        cols = slice(which * BLOCK, (which + 1) * BLOCK)
        low, high = (resp_ref[i : i + 16, cols, :].reshape(RESP // 2, HDIM) for i in (0, 16))
        return jnp.concatenate([high, low] if FLIP_RESP else [low, high], axis=0)

    queries = take(0)
    k_s[PROMPT:, :] = take(1)
    v_s[PROMPT:, :] = take(2)
    gain = adv_ref[me]
    length = len_ref[me]
    row = lax.broadcasted_iota(jnp.int32, (RESP, HDIM), 0)
    weight = jnp.where(row < length, gain, 0.0)
    cot = take(3)
    grad = (cot.astype(F32) * weight).astype(BF16)

    power = jnp.full((8, HDIM), head + 1, jnp.int32).astype(F32) * (-8.0 / HEADS)
    slope = (jnp.exp2(power) * (128.0 / (PROMPT + RESP) * LOG2E))[0:1, :]
    key_row = lax.broadcasted_iota(jnp.int32, (CHUNK, HDIM), 0)
    block = jnp.bitwise_xor(key_row // 8, FLIP_IN % 32)
    prompt_row = ((block // 8) * 256 + (block % 8) * 8 + key_row % 8 - PROMPT).astype(F32)
    resp_row = key_row.astype(F32)

    def wide4(x):
        return jnp.concatenate([x] * 4, axis=1)

    top = jnp.full((8, RESP), -jnp.inf, F32)
    for c in range(n_chunks):
        rows = slice(c * CHUNK, (c + 1) * CHUNK)
        if c < n_prompt:
            dc, dx, half = c % 2, (c // 2) % 2, c // 4
            both = parts[dc][dx][half * 32 : (half + 1) * 32].astype(F32)
            place = (half ^ (FLIP_IN // 32)) * 1024 + jnp.bitwise_xor(x, dx) * 128 + jnp.bitwise_xor(core, dc) * 64
            k_s[rows, :] = both[:, 0:8, :].reshape(CHUNK, HDIM).astype(BF16)
            v_s[rows, :] = both[:, 8:16, :].reshape(CHUNK, HDIM).astype(BF16)
            bias = slope * (prompt_row + place.astype(F32))
        else:
            bias = slope * (resp_row + float((c - n_prompt) * CHUNK))
        scores = dot(k_s[rows, :], queries, 1, 1)
        t = scores * (factor * LOG2E) + wide4(bias)
        if c >= n_prompt:
            key_pos = lax.broadcasted_iota(jnp.int32, (CHUNK, RESP), 0) + (c - n_prompt) * CHUNK
            query_pos = lax.broadcasted_iota(jnp.int32, (CHUNK, RESP), 1)
            t = jnp.where(key_pos <= query_pos, t, -jnp.inf)
        t_s[rows, :] = t
        top = jnp.maximum(top, jnp.max(t.reshape(CHUNK // 8, 8, RESP), axis=0))
    top = jnp.max(top, axis=0, keepdims=True)

    total = jnp.zeros((8, RESP), F32)
    delta = jnp.zeros((8, RESP), F32)
    for c in range(n_chunks):
        rows = slice(c * CHUNK, (c + 1) * CHUNK)
        p = jnp.exp2(t_s[rows, :] - top)
        t_s[rows, :] = p
        dp = dot(v_s[rows, :], grad, 1, 1)
        d_s[rows, :] = dp
        total = total + jnp.sum(p.reshape(CHUNK // 8, 8, RESP), axis=0)
        delta = delta + jnp.sum((p * dp).reshape(CHUNK // 8, 8, RESP), axis=0)
    inv = 1.0 / jnp.sum(total, axis=0, keepdims=True)
    delta = jnp.sum(delta, axis=0, keepdims=True) * inv

    def store_blocks(z, which, rows):
        count = rows.shape[0] // (4 * BLOCK)
        rows = rows.astype(BF16).reshape(count, 4, BLOCK, HDIM)
        for xt in range(2):
            for ct in range(2):
                for i in range(0, count, 4):
                    at = (z + i) ^ (FLIP_BACK // 2)
                    mine_ref[
                        at : at + 4,
                        ct,
                        jnp.bitwise_xor(x, xt),
                        which * BLOCK : (which + 1) * BLOCK,
                        :,
                    ] = rows[i : i + 4, xt * 2 + ct]

    dq = jnp.zeros((HDIM, RESP), F32)
    for c in range(n_chunks):
        rows = slice(c * CHUNK, (c + 1) * CHUNK)
        p = t_s[rows, :] * inv
        ds = (p * (d_s[rows, :] - delta)).astype(BF16)
        dv = dot(p.astype(BF16), grad, 1, 0)
        dk = dot(ds, queries, 1, 0) * factor
        dq = dq + dot(k_s[rows, :], ds, 0, 0)
        if c < n_prompt:
            both = jnp.concatenate(
                [dk.reshape(CHUNK // 8, 8, HDIM), dv.reshape(CHUNK // 8, 8, HDIM)], axis=1
            ).astype(BF16)
            out = send_ref if c % 2 else keep_ref
            for i in range(32):
                out[(c // 2) % 2, (c // 4 * 32 + i) ^ FLIP_IN ^ FLIP_OUT] = both[i]
        else:
            store_blocks((c - n_prompt) * 4, 1, dk)
            store_blocks((c - n_prompt) * 4, 2, dv)
    store_blocks(0, 0, (dq * factor).T)


def add_core_kernel(keep_ref, got_ref, next_ref, send_ref):
    next_ref[...] = (keep_ref[0].astype(F32) + got_ref[0].astype(F32)).astype(BF16)
    send_ref[...] = (keep_ref[1].astype(F32) + got_ref[1].astype(F32)).astype(BF16)


def add_x_kernel(keep_ref, got_ref, out_ref):
    out_ref[...] = (keep_ref[...].astype(F32) + got_ref[...].astype(F32)).astype(BF16)


def split_x_kernel(got_ref, out_ref):
    out_ref[...] = got_ref[:, :, 1]


def unpack_resp_kernel(got_ref, from_x_ref, q_ref, k_ref, v_ref):
    x = lax.axis_index("x")
    for z in range(8):
        h = z // 2
        for dx in range(2):
            for c in range(2):
                r = (z % 2) * 4 + jnp.bitwise_xor(x, dx) * 2 + c
                at = z ^ (FLIP_BACK // 2)
                rows = from_x_ref[at, c] if dx else got_ref[at, c, 0]
                for i, ref in enumerate((q_ref, k_ref, v_ref)):
                    ref[r, :, h * HDIM : (h + 1) * HDIM] = rows[i * BLOCK : (i + 1) * BLOCK]


def unpack_prompt_kernel(got_ref, k_ref, v_ref):
    for zh in range(4):
        for n in range(8):
            cols = slice((n * 4 + zh) * HDIM, (n * 4 + zh + 1) * HDIM)
            both = (
                got_ref[(zh * 16 + n) ^ FLIP_OUT].astype(F32)
                + got_ref[(zh * 16 + 8 + n) ^ FLIP_OUT].astype(F32)
            )
            k_ref[:, cols] = both[0:8].astype(BF16)
            v_ref[:, cols] = both[8:16].astype(BF16)


def groups_of(axes, flip):
    sizes = dict(zip(AXES, (4, 2, 2, 2, 8)))
    ids = np.arange(256).reshape([sizes[a] for a in AXES])
    rest = [a for a in AXES if a not in axes]
    ids = ids.transpose([AXES.index(a) for a in rest + list(axes)])
    ids = ids.reshape(-1, math.prod(sizes[a] for a in axes))
    return ids[:, np.arange(ids.shape[1]) ^ flip].tolist()


def exchange(x, axes, flip):
    return lax.all_to_all(
        x, AXES, 0, 0, axis_index_groups=groups_of(axes, flip), tiled=True
    )


def call(kernel, outs, n_in, scratch=(), smem=0, params=PARAMS, flops=0, bytes_accessed=1 << 20):
    return pl.pallas_call(
        kernel,
        out_shape=[jax.ShapeDtypeStruct(s, BF16) for s in outs],
        in_specs=[SMEM] * smem + [VMEM] * n_in,
        out_specs=[VMEM] * len(outs),
        scratch_shapes=list(scratch),
        compiler_params=params,
        cost_estimate=pl.CostEstimate(
            flops=flops, bytes_accessed=bytes_accessed, transcendentals=0
        ),
    )


def body(resp_q, resp_k, resp_v, resp_dout, advantage, resp_len, prompt_k, prompt_v):
    swap = [(0, 1), (1, 0)]
    (sent_p,) = call(pack_prompt_kernel, [(64, 16, HDIM)], 2, params=None)(prompt_k, prompt_v)
    p00 = exchange(sent_p, ("zh", "zl", "narrow"), FLIP_IN)
    p01 = lax.ppermute(p00, "x", swap)
    p10 = lax.ppermute(p00, "core", swap)
    p11 = lax.ppermute(p01, "core", swap)
    (sent_r,) = call(pack_resp_kernel, [(32, 4 * BLOCK, HDIM)], 4)(
        resp_q, resp_k, resp_v, resp_dout
    )
    got_r = exchange(sent_r, WIDE, FLIP_RESP)

    keys = PROMPT + RESP
    mine, keep, send = call(
        attn_kernel,
        [(8, 2, 2, 3 * BLOCK, HDIM), (2, 64, 16, HDIM), (2, 64, 16, HDIM)],
        5,
        scratch=[
            pltpu.VMEM((keys, HDIM), BF16),
            pltpu.VMEM((keys, HDIM), BF16),
            pltpu.VMEM((keys, RESP), F32),
            pltpu.VMEM((keys, RESP), F32),
        ],
        smem=2,
        flops=5 * 2 * keys * RESP * HDIM,
        bytes_accessed=3 << 20,
    )(advantage, resp_len, got_r, p00, p01, p10, p11)

    got = lax.ppermute(send, "core", swap)
    keep, send = call(add_core_kernel, [(64, 16, HDIM)] * 2, 2)(keep, got)
    got = lax.ppermute(send, "x", swap)
    back = exchange(mine.reshape(16, 2, 3 * BLOCK, HDIM), ("zh", "zl", "core"), FLIP_BACK)
    back = back.reshape(8, 2, 2, 3 * BLOCK, HDIM)
    (owned,) = call(add_x_kernel, [(64, 16, HDIM)], 2)(keep, got)
    owned, _ = lax.optimization_barrier((owned, back))
    owned = exchange(owned, ("zh", "zl", "narrow"), FLIP_OUT)
    (part,) = call(split_x_kernel, [(8, 2, 3 * BLOCK, HDIM)], 1)(back)
    from_x = lax.ppermute(part, "x", swap)
    grad_q, grad_k, grad_v = call(unpack_resp_kernel, [(RESPONSES, BLOCK, 4 * HDIM)] * 3, 2)(
        back, from_x
    )
    prompt_gk, prompt_gv = call(unpack_prompt_kernel, [(8, HEADS * HDIM)] * 2, 1)(
        owned
    )
    return grad_q, grad_k, grad_v, prompt_gk, prompt_gv


def solution(mesh):
    fine = Mesh(mesh.devices.reshape(4, 2, 2, 2, 8), AXES)
    resp = P(None, WIDE, "narrow")
    prompt = P(AXES, None)
    return jax.shard_map(
        body,
        mesh=fine,
        in_specs=(resp, resp, resp, resp, P(), P(), prompt, prompt),
        out_specs=(resp, resp, resp, prompt, prompt),
        check_vma=False,
    )
```

```python
import functools
import math

import jax
import jax.numpy as jnp
import numpy as np
from jax import lax
from jax.experimental import pallas as pl
from jax.experimental.pallas import tpu as pltpu
from jax.sharding import Mesh, PartitionSpec as P

HEADS = 32
HDIM = 128
RESPONSES = 8
RESP = 512
PROMPT = 2048
BLOCK = 16
CHUNK = 256
FLIP_IN, FLIP_RESP, FLIP_BACK, FLIP_OUT = 37, 16, 8, 32
LOG2E = 1.4426950408889634
F32 = jnp.float32
BF16 = jnp.bfloat16

AXES = ("zh", "zl", "x", "core", "narrow")
WIDE = ("zh", "zl", "x", "core")
GROUP = ("zl", "x", "core")

VMEM = pl.BlockSpec(memory_space=pltpu.VMEM)
SMEM = pl.BlockSpec(memory_space=pltpu.SMEM)
PARAMS = pltpu.CompilerParams(vmem_limit_bytes=48 * 1024 * 1024)


def pack_prompt_kernel(k_ref, v_ref, out_ref):
    keys = k_ref[...].astype(F32)
    values = v_ref[...].astype(F32)
    for zh in range(4):
        for n in range(8):
            cols = slice((n * 4 + zh) * HDIM, (n * 4 + zh + 1) * HDIM)
            both = jnp.concatenate([keys[:, cols], values[:, cols]], axis=0)
            both = both.astype(BF16)
            out_ref[(zh * 16 + n) ^ FLIP_IN] = both
            out_ref[(zh * 16 + 8 + n) ^ FLIP_IN] = both


def pack_resp_kernel(q_ref, k_ref, v_ref, o_ref, out_ref):
    for h in range(4):
        for r in range(RESPONSES):
            for i, ref in enumerate((q_ref, k_ref, v_ref, o_ref)):
                out_ref[(h * 8 + r) ^ FLIP_RESP, i * BLOCK : (i + 1) * BLOCK, :] = ref[
                    r, :, h * HDIM : (h + 1) * HDIM
                ]


def dot(a, b, ca, cb):
    return lax.dot_general(a, b, (((ca,), (cb,)), ((), ())), preferred_element_type=F32)


def attn_kernel(
    adv_ref, len_ref, resp_ref, p00_ref, p01_ref, p10_ref, p11_ref,
    mine_ref, keep_ref, send_ref,
    k_s, v_s, t_s, d_s,
):
    me = lax.axis_index(GROUP)
    core = lax.axis_index("core")
    x = lax.axis_index("x")
    parts = ((p00_ref, p01_ref), (p10_ref, p11_ref))
    head = lax.axis_index("narrow") * 4 + lax.axis_index("zh")
    factor = HDIM ** -0.5
    n_prompt = PROMPT // CHUNK
    n_chunks = (PROMPT + RESP) // CHUNK

    def take(which):
        cols = slice(which * BLOCK, (which + 1) * BLOCK)
        low, high = (resp_ref[i : i + 16, cols, :].reshape(RESP // 2, HDIM) for i in (0, 16))
        return jnp.concatenate([high, low] if FLIP_RESP else [low, high], axis=0)

    queries = take(0)
    k_s[PROMPT:, :] = take(1)
    v_s[PROMPT:, :] = take(2)
    gain = adv_ref[me]
    length = len_ref[me]
    row = lax.broadcasted_iota(jnp.int32, (RESP, HDIM), 0)
    weight = jnp.where(row < length, gain, 0.0)
    cot = take(3)
    grad = (cot.astype(F32) * weight).astype(BF16)

    power = jnp.full((8, HDIM), head + 1, jnp.int32).astype(F32) * (-8.0 / HEADS)
    slope = (jnp.exp2(power) * (128.0 / (PROMPT + RESP) * LOG2E))[0:1, :]
    key_row = lax.broadcasted_iota(jnp.int32, (CHUNK, HDIM), 0)
    block = jnp.bitwise_xor(key_row // 8, FLIP_IN % 32)
    prompt_row = ((block // 8) * 256 + (block % 8) * 8 + key_row % 8 - PROMPT).astype(F32)
    resp_row = key_row.astype(F32)

    def wide4(x):
        return jnp.concatenate([x] * 4, axis=1)

    top = jnp.full((8, RESP), -jnp.inf, F32)
    for c in range(n_chunks):
        rows = slice(c * CHUNK, (c + 1) * CHUNK)
        if c < n_prompt:
            dc, dx, half = c % 2, (c // 2) % 2, c // 4
            both = parts[dc][dx][half * 32 : (half + 1) * 32].astype(F32)
            place = (half ^ (FLIP_IN // 32)) * 1024 + jnp.bitwise_xor(x, dx) * 128 + jnp.bitwise_xor(core, dc) * 64
            k_s[rows, :] = both[:, 0:8, :].reshape(CHUNK, HDIM).astype(BF16)
            v_s[rows, :] = both[:, 8:16, :].reshape(CHUNK, HDIM).astype(BF16)
            bias = slope * (prompt_row + place.astype(F32))
        else:
            bias = slope * (resp_row + float((c - n_prompt) * CHUNK))
        scores = dot(k_s[rows, :], queries, 1, 1)
        t = scores * (factor * LOG2E) + wide4(bias)
        if c >= n_prompt:
            key_pos = lax.broadcasted_iota(jnp.int32, (CHUNK, RESP), 0) + (c - n_prompt) * CHUNK
            query_pos = lax.broadcasted_iota(jnp.int32, (CHUNK, RESP), 1)
            t = jnp.where(key_pos <= query_pos, t, -jnp.inf)
        t_s[rows, :] = t
        top = jnp.maximum(top, jnp.max(t.reshape(CHUNK // 8, 8, RESP), axis=0))
    top = jnp.max(top, axis=0, keepdims=True)

    total = jnp.zeros((8, RESP), F32)
    delta = jnp.zeros((8, RESP), F32)
    for c in range(n_chunks):
        rows = slice(c * CHUNK, (c + 1) * CHUNK)
        p = jnp.exp2(t_s[rows, :] - top)
        t_s[rows, :] = p
        dp = dot(v_s[rows, :], grad, 1, 1)
        d_s[rows, :] = dp
        total = total + jnp.sum(p.reshape(CHUNK // 8, 8, RESP), axis=0)
        delta = delta + jnp.sum((p * dp).reshape(CHUNK // 8, 8, RESP), axis=0)
    inv = 1.0 / jnp.sum(total, axis=0, keepdims=True)
    delta = jnp.sum(delta, axis=0, keepdims=True) * inv

    def store_blocks(z, which, rows):
        count = rows.shape[0] // (4 * BLOCK)
        rows = rows.astype(BF16).reshape(count, 4, BLOCK, HDIM)
        for xt in range(2):
            for ct in range(2):
                for i in range(0, count, 4):
                    at = (z + i) ^ (FLIP_BACK // 2)
                    mine_ref[
                        at : at + 4,
                        ct,
                        jnp.bitwise_xor(x, xt),
                        which * BLOCK : (which + 1) * BLOCK,
                        :,
                    ] = rows[i : i + 4, xt * 2 + ct]

    dq = jnp.zeros((HDIM, RESP), F32)
    for c in range(n_chunks):
        rows = slice(c * CHUNK, (c + 1) * CHUNK)
        p = t_s[rows, :] * inv
        ds = (p * (d_s[rows, :] - delta)).astype(BF16)
        dv = dot(p.astype(BF16), grad, 1, 0)
        dk = dot(ds, queries, 1, 0) * factor
        dq = dq + dot(k_s[rows, :], ds, 0, 0)
        if c < n_prompt:
            both = jnp.concatenate(
                [dk.reshape(CHUNK // 8, 8, HDIM), dv.reshape(CHUNK // 8, 8, HDIM)], axis=1
            ).astype(BF16)
            out = send_ref if c % 2 else keep_ref
            for i in range(32):
                out[(c // 2) % 2, (c // 4 * 32 + i) ^ FLIP_IN ^ FLIP_OUT] = both[i]
        else:
            store_blocks((c - n_prompt) * 4, 1, dk)
            store_blocks((c - n_prompt) * 4, 2, dv)
    store_blocks(0, 0, (dq * factor).T)


def add_core_kernel(keep_ref, got_ref, next_ref, send_ref):
    next_ref[...] = (keep_ref[0].astype(F32) + got_ref[0].astype(F32)).astype(BF16)
    send_ref[...] = (keep_ref[1].astype(F32) + got_ref[1].astype(F32)).astype(BF16)


def add_x_kernel(keep_ref, got_ref, out_ref):
    out_ref[...] = (keep_ref[...].astype(F32) + got_ref[...].astype(F32)).astype(BF16)


def split_x_kernel(got_ref, out_ref):
    out_ref[...] = got_ref[:, :, 1]


def unpack_resp_kernel(got_ref, from_x_ref, q_ref, k_ref, v_ref):
    x = lax.axis_index("x")
    for z in range(8):
        h = z // 2
        for dx in range(2):
            for c in range(2):
                r = (z % 2) * 4 + jnp.bitwise_xor(x, dx) * 2 + c
                at = z ^ (FLIP_BACK // 2)
                rows = from_x_ref[at, c] if dx else got_ref[at, c, 0]
                for i, ref in enumerate((q_ref, k_ref, v_ref)):
                    ref[r, :, h * HDIM : (h + 1) * HDIM] = rows[i * BLOCK : (i + 1) * BLOCK]


def unpack_prompt_kernel(got_ref, k_ref, v_ref):
    for zh in range(4):
        for n in range(8):
            cols = slice((n * 4 + zh) * HDIM, (n * 4 + zh + 1) * HDIM)
            both = (
                got_ref[(zh * 16 + n) ^ FLIP_OUT].astype(F32)
                + got_ref[(zh * 16 + 8 + n) ^ FLIP_OUT].astype(F32)
            )
            k_ref[:, cols] = both[0:8].astype(BF16)
            v_ref[:, cols] = both[8:16].astype(BF16)


def groups_of(axes, flip):
    sizes = dict(zip(AXES, (4, 2, 2, 2, 8)))
    ids = np.arange(256).reshape([sizes[a] for a in AXES])
    rest = [a for a in AXES if a not in axes]
    ids = ids.transpose([AXES.index(a) for a in rest + list(axes)])
    ids = ids.reshape(-1, math.prod(sizes[a] for a in axes))
    return ids[:, np.arange(ids.shape[1]) ^ flip].tolist()


def exchange(x, axes, flip):
    return lax.all_to_all(
        x, AXES, 0, 0, axis_index_groups=groups_of(axes, flip), tiled=True
    )


def call(kernel, outs, n_in, scratch=(), smem=0, params=PARAMS, flops=0, bytes_accessed=1 << 20):
    return pl.pallas_call(
        kernel,
        out_shape=[jax.ShapeDtypeStruct(s, BF16) for s in outs],
        in_specs=[SMEM] * smem + [VMEM] * n_in,
        out_specs=[VMEM] * len(outs),
        scratch_shapes=list(scratch),
        compiler_params=params,
        cost_estimate=pl.CostEstimate(
            flops=flops, bytes_accessed=bytes_accessed, transcendentals=0
        ),
    )


def body(resp_q, resp_k, resp_v, resp_dout, advantage, resp_len, prompt_k, prompt_v):
    swap = [(0, 1), (1, 0)]
    (sent_p,) = call(pack_prompt_kernel, [(64, 16, HDIM)], 2, params=None)(prompt_k, prompt_v)
    p00 = exchange(sent_p, ("zh", "zl", "narrow"), FLIP_IN)
    p01 = lax.ppermute(p00, "x", swap)
    p10 = lax.ppermute(p00, "core", swap)
    p11 = lax.ppermute(p01, "core", swap)
    (sent_r,) = call(pack_resp_kernel, [(32, 4 * BLOCK, HDIM)], 4)(
        resp_q, resp_k, resp_v, resp_dout
    )
    got_r = exchange(sent_r, WIDE, FLIP_RESP)

    keys = PROMPT + RESP
    mine, keep, send = call(
        attn_kernel,
        [(8, 2, 2, 3 * BLOCK, HDIM), (2, 64, 16, HDIM), (2, 64, 16, HDIM)],
        5,
        scratch=[
            pltpu.VMEM((keys, HDIM), BF16),
            pltpu.VMEM((keys, HDIM), BF16),
            pltpu.VMEM((keys, RESP), F32),
            pltpu.VMEM((keys, RESP), F32),
        ],
        smem=2,
        flops=5 * 2 * keys * RESP * HDIM,
        bytes_accessed=3 << 20,
    )(advantage, resp_len, got_r, p00, p01, p10, p11)

    got = lax.ppermute(send, "core", swap)
    keep, send = call(add_core_kernel, [(64, 16, HDIM)] * 2, 2)(keep, got)
    got = lax.ppermute(send, "x", swap)
    back = exchange(mine.reshape(16, 2, 3 * BLOCK, HDIM), ("zh", "zl", "core"), FLIP_BACK)
    back = back.reshape(8, 2, 2, 3 * BLOCK, HDIM)
    (owned,) = call(add_x_kernel, [(64, 16, HDIM)], 2)(keep, got)
    owned, _ = lax.optimization_barrier((owned, back))
    owned = exchange(owned, ("zh", "zl", "narrow"), FLIP_OUT)
    (part,) = call(split_x_kernel, [(8, 2, 3 * BLOCK, HDIM)], 1)(back)
    from_x = lax.ppermute(part, "x", swap)
    grad_q, grad_k, grad_v = call(unpack_resp_kernel, [(RESPONSES, BLOCK, 4 * HDIM)] * 3, 2)(
        back, from_x
    )
    prompt_gk, prompt_gv = call(unpack_prompt_kernel, [(8, HEADS * HDIM)] * 2, 1)(
        owned
    )
    return grad_q, grad_k, grad_v, prompt_gk, prompt_gv


def solution(mesh):
    fine = Mesh(mesh.devices.reshape(4, 2, 2, 2, 8), AXES)
    resp = P(None, WIDE, "narrow")
    prompt = P(AXES, None)
    return jax.shard_map(
        body,
        mesh=fine,
        in_specs=(resp, resp, resp, resp, P(), P(), prompt, prompt),
        out_specs=(resp, resp, resp, prompt, prompt),
        check_vma=False,
    )
```
